768 devices in a mesh: rep: 48 (over z, x_hi, core), shard: 16 (over x_lo, y).
Axes of the slice: x: 4 (x_hi: 2, x_lo: 2; x = x_hi * 2 + x_lo), y: 8, z: 12, core: 2. Of those that a mesh axis runs over, the one named last changes fastest.
Arguments:
- seq_lengths: int32 [768, 2], P(('rep', 'shard')), may hold values from 1 to 64, as said below
- token_ids: int32 [98304], P(('rep', 'shard')), may hold values from 4 to 28
- masked: int32 [98304], P(('rep', 'shard')), may hold values 0 or 1
- embed_table: bfloat16 [33, 5120], replicated
- ln_gain: float32 [5120], replicated, may hold values from 0.25 to 4
- grad_resid: bfloat16 [98304, 5120], P(('rep', 'shard')), may hold values from -0.1875 to 0.1875
- grad_normed: bfloat16 [98304, 5120], P(('rep', 'shard')), may hold values from -0.1875 to 0.1875
Outputs:
- layer_grads: float32 [15360], P('shard')
- embed_grads: float32 [168960], P('shard')
The draws below stay inside these ranges and needn't reach their ends.
Inputs may be any that keep to these rules, and one draw needn't show every extreme that they name: `seq_lengths`: on every device one of its sequences has length exactly 64; the others have lengths of 1 to 64.
All inputs are finite; a program needn't handle non-finite values. No bound on the sum of `masked` on one device may be relied on, other than what follows from the above.
Results may differ from the reference program's by a relative error of at most 0.0003.
Values sent between devices are 32-bit elements; how exact they have to be, the bound alone decides.
No kernel may reach another device: no remote copies, remote signals or barrier semaphores. Data moves between devices by JAX's collectives and lax.ppermute only.
A program may use at most 32 MiB of HBM per device.

```python
import math
import jax
import jax.numpy as jnp
from jax import lax

D = 5120
VOCAB = 33
SEQ_DEV = 2
MOST = 64
HOLDERS = 768
TOKENS = 98304


def draw_seq_lengths(key, part):
    key = jax.random.fold_in(key, 11)
    key_first, key_second, key_full = jax.random.split(key, 3)
    first_draw = jax.random.randint(key_first, (HOLDERS, SEQ_DEV), 1, MOST + 1)
    second_draw = jax.random.randint(key_second, (HOLDERS, SEQ_DEV), 1, MOST + 1)
    shorter = jnp.minimum(first_draw, second_draw)
    full_slot = jax.random.randint(key_full, (HOLDERS, 1), 0, SEQ_DEV)
    slot_index = jnp.arange(SEQ_DEV, dtype=jnp.int32)[None, :]
    return jnp.where(slot_index == full_slot, MOST, shorter).astype(jnp.int32)


def draw_embed_table(key, part):
    key = jax.random.fold_in(key, 23)
    key_values, key_rows, key_cols = jax.random.split(key, 3)
    entries = jnp.clip(jax.random.normal(key_values, (VOCAB, D), jnp.float32), -6.0, 6.0)
    row_scale = jnp.exp(jax.random.uniform(key_rows, (VOCAB, 1), jnp.float32, 0.0, math.log(3.2)))
    col_scale = jnp.exp(jax.random.uniform(key_cols, (1, D), jnp.float32, 0.0, math.log(3.2)))
    return (entries * row_scale * col_scale).astype(jnp.bfloat16)


def with_ends(array, own_key, low, top_value):
    dims = array.shape
    index_at = [jax.random.randint(jax.random.fold_in(own_key, axis), (), 0, dims[axis]) for axis in range(len(dims))]
    array = array.at[tuple(index_at)].set(low)
    longest = dims.index(max(dims))
    index_at[longest] = (index_at[longest] + 1) % dims[longest]
    return array.at[tuple(index_at)].set(top_value)


def levels(own_key, extent, pieces, low, high):
    gain, own = 1.0, jax.random.fold_in(own_key, 6)
    for axis_at, blocks in pieces:
        draws = jnp.exp(jax.random.uniform(jax.random.fold_in(own, axis_at), (blocks,), jnp.float32, low / len(pieces), high / len(pieces)))
        gain = gain * jnp.repeat(draws, extent[axis_at] // blocks).reshape([-1 if axis == axis_at else 1 for axis in range(len(extent))])
    return gain


def gaussian(rng, shape, deviation, bound, cuts=(), kind=jnp.bfloat16):
    values = deviation * jax.random.normal(rng, shape, jnp.float32)
    if cuts:
        values = values * levels(rng, shape, cuts, -0.22, 0.18)
    return jnp.clip(values, -bound, bound).astype(kind)


def setup_inputs(seed: int = 0) -> dict:
    key_of = jax.random.split(jax.random.key(seed), 8)
    return {
        "seq_lengths": draw_seq_lengths(jax.random.fold_in(key_of[7], 71), 0),
        "token_ids": with_ends(jax.random.randint(key_of[1], (TOKENS,), 4, 29), jax.random.fold_in(key_of[1], 1), 4, 28).astype(jnp.int32),
        "masked": with_ends((jax.random.randint(key_of[2], (TOKENS,), 0, 100) < 15).astype(jnp.int32), jax.random.fold_in(key_of[2], 1), 0, 1),
        "embed_table": draw_embed_table(jax.random.fold_in(key_of[7], 71), 0),
        "ln_gain": jnp.clip(jnp.exp(jax.random.uniform(key_of[4], (D,), jnp.float32, math.log(0.25), math.log(4.0))), 0.25, 4.0),
        "grad_resid": gaussian(key_of[5], (TOKENS, D), (4.0 / (TOKENS ** 0.5)), 0.1875, ((0, 768),)),
        "grad_normed": gaussian(key_of[6], (TOKENS, D), (4.0 / (TOKENS ** 0.5)), 0.1875, ((0, 768),)),
    }


def token_weights(lengths, masked):
    slot_count = masked.shape[0]
    seq_ends = jnp.cumsum(lengths)
    seq_starts = seq_ends - lengths
    position = jnp.arange(slot_count, dtype=jnp.int32)[:, None]
    member = ((position >= seq_starts[None, :]) & (position < seq_ends[None, :])).astype(jnp.float32)
    masked_f = masked.astype(jnp.float32)
    masked_count = lax.optimization_barrier(jnp.sum(member * masked_f[:, None], axis=0))
    mask_ratio = masked_count / lengths.astype(jnp.float32)
    factor = 0.88 / jnp.maximum(1.0 - mask_ratio, 0.5)
    live_rows = lax.optimization_barrier(jnp.sum(member, axis=1))
    token_scale = lax.optimization_barrier(jnp.sum(member * factor[None, :], axis=1))
    return (live_rows, live_rows * (1.0 - masked_f) * token_scale)

def device_grads(lengths, token_ids, masked, embed_table, ln_gain, grad_resid, grad_normed):
    live_rows, weight = token_weights(lengths, masked)
    vocab_size = embed_table.shape[0]
    onehot = (token_ids[:, None] == jnp.arange(vocab_size, dtype=jnp.int32)[None, :]).astype(jnp.bfloat16)
    looked_up = jnp.dot(onehot, embed_table, preferred_element_type=jnp.float32)
    embedded = looked_up * weight[:, None]
    row_mean = lax.optimization_barrier(jnp.mean(embedded, axis=1, keepdims=True))
    centered = embedded - row_mean
    inv_std = lax.rsqrt(lax.optimization_barrier(jnp.mean(centered * centered, axis=1, keepdims=True)) + 1e-05)
    normed = centered * inv_std
    resid_cot = grad_resid.astype(jnp.float32) * live_rows[:, None]
    normed_cot = grad_normed.astype(jnp.float32) * live_rows[:, None]
    layer_sums = jnp.stack([lax.optimization_barrier(jnp.sum(resid_cot, axis=0)), lax.optimization_barrier(jnp.sum(normed_cot * normed, axis=0)), lax.optimization_barrier(jnp.sum(normed_cot, axis=0))])
    scaled = normed_cot * ln_gain.astype(jnp.float32)[None, :]
    through = inv_std * (scaled - lax.optimization_barrier(jnp.mean(scaled, axis=1, keepdims=True)) - normed * lax.optimization_barrier(jnp.mean(scaled * normed, axis=1, keepdims=True)))
    flowing = (resid_cot + through) * weight[:, None]
    embed_sums = jnp.dot(onehot.astype(jnp.float32).T, flowing, precision=lax.Precision.HIGHEST)
    return (layer_sums, embed_sums)

def reference(seq_lengths, token_ids, masked, embed_table, ln_gain, grad_resid, grad_normed):
    device_count = seq_lengths.shape[0]
    ids_all = token_ids.reshape(device_count, -1)
    masks_all = masked.reshape(device_count, -1)
    resid_all = grad_resid.reshape(device_count, -1, D)
    normed_all = grad_normed.reshape(device_count, -1, D)

    def scan_step(totals, device_item):
        lengths, ids_here, mask_here, resid_here, normed_here = device_item
        layer_sums, embed_sums = device_grads(lengths, ids_here, mask_here, embed_table, ln_gain, resid_here, normed_here)
        return ((totals[0] + layer_sums, totals[1] + embed_sums), None)
    zeros_init = (jnp.zeros((3, D), jnp.float32), jnp.zeros((VOCAB, D), jnp.float32))
    (layer_total, embed_total), _ = lax.scan(scan_step, zeros_init, (seq_lengths, ids_all, masks_all, resid_all, normed_all))
    return (layer_total.reshape(-1), embed_total.reshape(-1))
```

```python
import jax
import jax.numpy as jnp
from jax import lax
from jax.sharding import Mesh
from jax.sharding import PartitionSpec as P

LANES = 128
SHARD = ("xl", "y")
HOLDERS = ("z4", "z3", "xh", "core", "xl", "y")


def token_weights(lengths, masked):
    slot_count = masked.shape[0]
    seq_ends = jnp.cumsum(lengths)
    seq_starts = seq_ends - lengths
    position = jnp.arange(slot_count, dtype=jnp.int32)[:, None]
    member = ((position >= seq_starts[None, :]) & (position < seq_ends[None, :])).astype(
        jnp.float32
    )
    masked_f = masked.astype(jnp.float32)
    masked_count = jnp.sum(member * masked_f[:, None], axis=0)
    mask_ratio = masked_count / lengths.astype(jnp.float32)
    factor = 0.88 / jnp.maximum(1.0 - mask_ratio, 0.5)
    live_rows = jnp.sum(member, axis=1)
    token_scale = jnp.sum(member * factor[None, :], axis=1)
    return (live_rows, live_rows * (1.0 - masked_f) * token_scale)


def exchange_sum(block, axes, count):
    sent = jnp.broadcast_to(block[None], (count, *block.shape))
    return lax.all_to_all(sent, axes, 0, 0, tiled=True)


def reduce_pieces(pieces):
    half = pieces.shape[1] // 2
    core = lax.axis_index("core")
    kept = lax.dynamic_slice_in_dim(pieces, core * half, half, 1)
    given = lax.dynamic_slice_in_dim(pieces, (1 - core) * half, half, 1)
    pair = kept + lax.ppermute(given, "core", [(0, 1), (1, 0)])
    owned = jnp.sum(lax.all_to_all(pair, SHARD, 0, 0, tiled=True), axis=0)
    far = jnp.sum(exchange_sum(owned, "z4", 4), axis=0)
    near = exchange_sum(far, ("z3", "xh", "core"), 12)
    return jnp.sum(near.reshape(6, 2, half, LANES), axis=0).reshape(-1)


def embedding_sums(onehot, weight, resid_cot, normed_cot, normed, inv_std, ln_gain):
    scaled = normed_cot * ln_gain[None, :]
    through = inv_std * (
        scaled
        - jnp.mean(scaled, axis=1, keepdims=True)
        - normed * jnp.mean(scaled * normed, axis=1, keepdims=True)
    )
    flowing = (resid_cot + through) * weight[:, None]
    return jnp.dot(onehot.astype(jnp.float32).T, flowing, precision=lax.Precision.HIGHEST)


def on_device(seq_lengths, token_ids, masked, embed_table, ln_gain, grad_resid, grad_normed):
    live_rows, weight = token_weights(seq_lengths[0], masked)
    vocab_size, width = embed_table.shape
    onehot = (token_ids[:, None] == jnp.arange(vocab_size, dtype=jnp.int32)[None, :]).astype(
        jnp.bfloat16
    )
    looked_up = jnp.dot(onehot, embed_table, preferred_element_type=jnp.float32)
    embedded = looked_up * weight[:, None]
    row_mean = jnp.mean(embedded, axis=1, keepdims=True)
    centered = embedded - row_mean
    inv_std = lax.rsqrt(jnp.mean(centered * centered, axis=1, keepdims=True) + 1e-05)
    normed = centered * inv_std
    resid_cot = grad_resid.astype(jnp.float32) * live_rows[:, None]
    normed_cot = grad_normed.astype(jnp.float32) * live_rows[:, None]
    layer_sums = jnp.stack(
        [
            jnp.sum(resid_cot, axis=0),
            jnp.sum(normed_cot * normed, axis=0),
            jnp.sum(normed_cot, axis=0),
        ]
    )
    embed_sums = embedding_sums(onehot, weight, resid_cot, normed_cot, normed, inv_std, ln_gain)
    embed_part = vocab_size * width // 16
    layer_part = 3 * width // 16
    rows = -(-(embed_part + layer_part) // (LANES * 16)) * 16
    pad = rows * LANES - embed_part - layer_part
    pieces = jnp.concatenate(
        [
            embed_sums.reshape(16, embed_part),
            layer_sums.reshape(16, layer_part),
            jnp.zeros((16, pad), jnp.float32),
        ],
        axis=1,
    ).reshape(16, rows, LANES)
    mine = reduce_pieces(pieces)
    return (mine[embed_part : embed_part + layer_part], mine[:embed_part])


def solution(mesh):
    fine = Mesh(mesh.devices.reshape(4, 3, 2, 2, 2, 8), HOLDERS)
    in_specs = (
        P(HOLDERS, None),
        P(HOLDERS),
        P(HOLDERS),
        P(),
        P(),
        P(HOLDERS, None),
        P(HOLDERS, None),
    )
    out_specs = (P(SHARD), P(SHARD))
    return jax.shard_map(
        on_device, mesh=fine, in_specs=in_specs, out_specs=out_specs, check_vma=False
    )
```

```python
import jax
import jax.numpy as jnp
from jax import lax
from jax.experimental import pallas as pl
from jax.experimental.pallas import tpu as pltpu
from jax.sharding import Mesh
from jax.sharding import PartitionSpec as P

LANES = 128
SUBLANES = 8
EPS = 1e-05
SHRINK = 2.0**-8
WIDTH_STEP = 512
VOCAB_USED = 32
OWNERS = 16
QUARTERS = 4
PIECE = 24
HOLDERS = ("z", "xh", "core", "xl", "y")


def token_rows(lengths_ref, masked_ref):
    masked = masked_ref[...].astype(jnp.float32)
    position = lax.broadcasted_iota(jnp.int32, masked.shape, 1)
    first, second = lengths_ref[0, 0], lengths_ref[0, 1]
    members = (position < first, (position >= first) & (position < first + second))
    scale = jnp.zeros_like(masked)
    for member, length in zip(members, (first, second)):
        length_f = jnp.full((1, 1), length, jnp.int32).astype(jnp.float32)
        count = jnp.sum(jnp.where(member, masked, 0.0), axis=1, keepdims=True)
        factor = 0.88 / jnp.maximum(1.0 - count / length_f, 0.5)
        scale = jnp.where(member, factor, scale)
    live = jnp.where(members[0] | members[1], 1.0, 0.0)
    return live, live * (1.0 - masked) * scale


def split3(value):
    high = value.astype(jnp.bfloat16)
    rest = value - high.astype(jnp.float32)
    mid = rest.astype(jnp.bfloat16)
    low = (rest - mid.astype(jnp.float32)).astype(jnp.bfloat16)
    return [high, mid, low]


def sum3(parts, at):
    n = VOCAB_USED
    return parts[at : at + n] + parts[at + n : at + 2 * n] + parts[at + 2 * n : at + 3 * n]


def lane_fold(value):
    total = value[:, :LANES]
    for at in range(LANES, value.shape[1], LANES):
        total = total + value[:, at : at + LANES]
    return total


def sums_kernel(
    lengths_ref, ids_ref, masked_ref, table_ref, gain_ref, resid_ref, normed_ref,
    given_ref, kept_ref, total_ref, flat_ref,
):
    width = table_ref.shape[1]
    blocks = width // LANES
    live, weight = token_rows(lengths_ref, masked_ref)
    n, slots = VOCAB_USED, weight.shape[1]
    small = table_ref[0:n, :].astype(jnp.float32) * SHRINK
    mean = jnp.sum(small, axis=1, keepdims=True) / width
    small = small - mean
    spread = jnp.sum(small * small, axis=1, keepdims=True) / width
    variance = jnp.minimum(spread * SHRINK**-2, 1e38)
    unit = lax.rsqrt(variance + EPS)
    unscaled = (variance + EPS) * unit

    hit = ids_ref[...] == lax.broadcasted_iota(jnp.int32, (n, slots), 0)
    weighted = jnp.where(hit, weight, 0.0)
    through = weighted * lax.rsqrt(weight * weight * variance + EPS)
    ratio = through * unscaled
    row = lax.broadcasted_iota(jnp.int32, (16, slots), 0)
    alive = jnp.where(row == 0, live, 0.0).astype(jnp.bfloat16)
    left_resid = jnp.concatenate([*split3(weighted), alive], axis=0)
    left_normed = jnp.concatenate(
        [*split3(through), *split3(through * ratio * ratio), alive], axis=0
    )

    mean_sum = jnp.zeros((n, LANES), jnp.float32)
    slope_sum = jnp.zeros((n, LANES), jnp.float32)
    for at in range(0, width, WIDTH_STEP):
        columns = slice(at, at + WIDTH_STEP)
        from_resid = jnp.dot(left_resid, resid_ref[:, columns], preferred_element_type=jnp.float32)
        from_normed = jnp.dot(
            left_normed, normed_ref[:, columns], preferred_element_type=jnp.float32
        )
        gain = gain_ref[:, columns]
        centered = table_ref[0:n, columns].astype(jnp.float32) * SHRINK - mean
        centered = centered * SHRINK**-1
        passed = sum3(from_normed, 0)
        gained = passed * gain
        mean_sum += lane_fold(gained)
        slope_sum += lane_fold(centered * unit * gain * sum3(from_normed, 3 * n))
        total_ref[:, columns] = sum3(from_resid, 0) + gained
        gain_grad = jnp.sum(centered * passed, axis=0, keepdims=True)
        row = lax.broadcasted_iota(jnp.int32, (SUBLANES, WIDTH_STEP), 0)
        layer = jnp.where(
            row == 1,
            from_resid[3 * n : 3 * n + 1],
            jnp.where(row == 2, gain_grad, jnp.where(row == 3, from_normed[6 * n : 6 * n + 1], 0.0)),
        )
        for k in range(WIDTH_STEP // LANES):
            at_row = n * blocks + at // LANES + k
            flat_ref[pl.ds(at_row, SUBLANES, stride=blocks), :] = layer[
                :, k * LANES : (k + 1) * LANES
            ]
    mean_sum = jnp.sum(mean_sum, axis=1, keepdims=True) / width
    slope = jnp.sum(slope_sum, axis=1, keepdims=True) / width * unit
    for k in range(blocks):
        columns = slice(k * LANES, (k + 1) * LANES)
        centered = table_ref[0:n, columns].astype(jnp.float32) * SHRINK - mean
        result = total_ref[:, columns] - mean_sum - centered * SHRINK**-1 * slope
        for tile in range(n // SUBLANES):
            rows = slice(tile * SUBLANES, (tile + 1) * SUBLANES)
            flat_ref[pl.ds(tile * SUBLANES * blocks + k, SUBLANES, stride=blocks), :] = result[rows]

    layer_row = (n + 1) * blocks

    def write(out_ref, core):
        for owner in range(OWNERS):
            for tile in range(PIECE * QUARTERS // SUBLANES):
                quarter, inner = divmod(tile, PIECE // SUBLANES)
                if quarter % 2 != core:
                    continue
                if tile == 0:
                    start = layer_row + owner * 15 // 2
                else:
                    start = owner * 165 // 2 + (tile - 1) * SUBLANES
                out_ref[quarter // 2 * OWNERS + owner, pl.ds(inner * SUBLANES, SUBLANES), :] = (
                    flat_ref[pl.ds(start, SUBLANES), :]
                )

    core = lax.axis_index("core")
    for value in range(2):

        @pl.when(core == value)
        def _():
            write(kept_ref, value)
            write(given_ref, 1 - value)


def local_sums(lengths, ids, masked, table, gain, resid, normed):
    width = table.shape[1]
    vmem = pl.BlockSpec(memory_space=pltpu.VMEM)
    smem = pl.BlockSpec(memory_space=pltpu.SMEM)
    out = jax.ShapeDtypeStruct((2 * OWNERS, PIECE, LANES), jnp.float32)
    return pl.pallas_call(
        sums_kernel,
        out_shape=(out, out),
        in_specs=[smem] + [vmem] * 6,
        out_specs=(vmem, vmem),
        scratch_shapes=[
            pltpu.VMEM((VOCAB_USED, width), jnp.float32),
            pltpu.VMEM(((VOCAB_USED + SUBLANES) * width // LANES, LANES), jnp.float32),
        ],
        compiler_params=pltpu.CompilerParams(vmem_limit_bytes=32 * 1024 * 1024),
        name="local_sums",
    )(lengths, ids[None], masked[None], table, gain[None], resid, normed)


def to_all(block, axes, count):
    sent = jnp.broadcast_to(block[None], (count, *block.shape))
    return lax.all_to_all(sent, axes, 0, 0, tiled=True)


def on_device(lengths, ids, masked, table, gain, resid, normed):
    given, kept = local_sums(lengths, ids, masked, table, gain, resid, normed)
    pair = kept + lax.ppermute(given, "core", [(0, 1), (1, 0)])
    piece = jnp.sum(lax.all_to_all(pair, ("xh", "xl", "y"), 0, 0, tiled=True), axis=0)
    piece = jnp.sum(to_all(piece, "z", 12), axis=0)
    owned = to_all(piece, ("xh", "core"), QUARTERS).reshape(-1)
    shift = (lax.axis_index("y") & 1) * (LANES // 2)
    layer = lax.dynamic_slice_in_dim(owned, shift, 3 * table.shape[1] // OWNERS)
    embed = lax.dynamic_slice_in_dim(
        owned, SUBLANES * LANES + shift, table.shape[0] * table.shape[1] // OWNERS
    )
    return layer, embed


def solution(mesh):
    fine = Mesh(mesh.devices.reshape(12, 2, 2, 2, 8), HOLDERS)
    in_specs = (
        P(HOLDERS, None),
        P(HOLDERS),
        P(HOLDERS),
        P(),
        P(),
        P(HOLDERS, None),
        P(HOLDERS, None),
    )
    owners = P(("xl", "y"))
    return jax.shard_map(
        on_device, mesh=fine, in_specs=in_specs, out_specs=(owners, owners), check_vma=False
    )
```

```python
import jax
import jax.numpy as jnp
from jax import lax
from jax.experimental import pallas as pl
from jax.experimental.pallas import tpu as pltpu
from jax.sharding import Mesh
from jax.sharding import PartitionSpec as P

LANES = 128
SUBLANES = 8
EPS = 1e-05
SHRINK = 2.0**-8
WIDTH_STEP = 512
COPY_STEP = 1024
VOCAB_USED = 32
OWNERS = 16
QUARTERS = 4
PIECE = 24
HOLDERS = ("z", "xh", "core", "xl", "y")


def token_rows(lengths_ref, masked_ref):
    masked = masked_ref[...].astype(jnp.float32)
    position = lax.broadcasted_iota(jnp.int32, masked.shape, 1)
    first, second = lengths_ref[0, 0], lengths_ref[0, 1]
    members = (position < first, (position >= first) & (position < first + second))
    scale = jnp.zeros_like(masked)
    for member, length in zip(members, (first, second)):
        length_f = jnp.full((1, 1), length, jnp.int32).astype(jnp.float32)
        count = jnp.sum(jnp.where(member, masked, 0.0), axis=1, keepdims=True)
        factor = 0.88 / jnp.maximum(1.0 - count / length_f, 0.5)
        scale = jnp.where(member, factor, scale)
    live = jnp.where(members[0] | members[1], 1.0, 0.0)
    return live, live * (1.0 - masked) * scale


def split3(value):
    high = value.astype(jnp.bfloat16)
    rest = value - high.astype(jnp.float32)
    mid = rest.astype(jnp.bfloat16)
    low = (rest - mid.astype(jnp.float32)).astype(jnp.bfloat16)
    return [high, mid, low]


def sum3(parts, at):
    n = VOCAB_USED
    return parts[at : at + n] + parts[at + n : at + 2 * n] + parts[at + 2 * n : at + 3 * n]


def lane_fold(value):
    total = value[:, :LANES]
    for at in range(LANES, value.shape[1], LANES):
        total = total + value[:, at : at + LANES]
    return total


def sums_kernel(
    lengths_hbm, ids_hbm, masked_hbm, table_hbm, gain_hbm, resid_hbm, normed_hbm,
    given_ref, kept_ref,
    lengths_ref, ids_ref, masked_ref, table_ref, gain_ref, resid_ref, normed_ref,
    total_ref, flat_ref, small_sem, resid_sem, normed_sem,
):
    small_copies = [
        pltpu.make_async_copy(source, target, small_sem.at[i])
        for i, (source, target) in enumerate(
            (
                (table_hbm, table_ref),
                (lengths_hbm, lengths_ref),
                (masked_hbm, masked_ref),
                (ids_hbm, ids_ref),
                (gain_hbm, gain_ref),
            )
        )
    ]
    large_copies = []
    for i in range(table_ref.shape[1] // COPY_STEP):
        columns = pl.ds(i * COPY_STEP, COPY_STEP)
        large_copies.append(
            [
                pltpu.make_async_copy(source.at[:, columns], target.at[:, columns], sem.at[i])
                for source, target, sem in (
                    (resid_hbm, resid_ref, resid_sem),
                    (normed_hbm, normed_ref, normed_sem),
                )
            ]
        )
    for copy in small_copies + sum(large_copies, []):
        copy.start()
    for copy in small_copies:
        copy.wait()
    width = table_ref.shape[1]
    blocks = width // LANES
    live, weight = token_rows(lengths_ref, masked_ref)
    n, slots = VOCAB_USED, weight.shape[1]
    small = table_ref[0:n, :].astype(jnp.float32) * SHRINK
    mean = jnp.sum(small, axis=1, keepdims=True) / width
    small = small - mean
    spread = jnp.sum(small * small, axis=1, keepdims=True) / width
    variance = jnp.minimum(spread * SHRINK**-2, 1e38)
    unit = lax.rsqrt(variance + EPS)
    unscaled = (variance + EPS) * unit

    hit = ids_ref[...] == lax.broadcasted_iota(jnp.int32, (n, slots), 0)
    weighted = jnp.where(hit, weight, 0.0)
    through = weighted * lax.rsqrt(weight * weight * variance + EPS)
    ratio = through * unscaled
    row = lax.broadcasted_iota(jnp.int32, (16, slots), 0)
    alive = jnp.where(row == 0, live, 0.0).astype(jnp.bfloat16)
    left_resid = jnp.concatenate([*split3(weighted), alive], axis=0)
    left_normed = jnp.concatenate(
        [*split3(through), *split3(through * ratio * ratio), alive], axis=0
    )

    mean_sum = jnp.zeros((n, LANES), jnp.float32)
    slope_sum = jnp.zeros((n, LANES), jnp.float32)
    for at in range(0, width, WIDTH_STEP):
        if at % COPY_STEP == 0:
            for copy in large_copies[at // COPY_STEP]:
                copy.wait()
        columns = slice(at, at + WIDTH_STEP)
        from_resid = jnp.dot(left_resid, resid_ref[:, columns], preferred_element_type=jnp.float32)
        from_normed = jnp.dot(
            left_normed, normed_ref[:, columns], preferred_element_type=jnp.float32
        )
        gain = gain_ref[:, columns]
        centered = table_ref[0:n, columns].astype(jnp.float32) * SHRINK - mean
        centered = centered * SHRINK**-1
        passed = sum3(from_normed, 0)
        gained = passed * gain
        mean_sum += lane_fold(gained)
        slope_sum += lane_fold(centered * unit * gain * sum3(from_normed, 3 * n))
        total_ref[:, columns] = sum3(from_resid, 0) + gained
        gain_grad = jnp.sum(centered * passed, axis=0, keepdims=True)
        row = lax.broadcasted_iota(jnp.int32, (SUBLANES, WIDTH_STEP), 0)
        layer = jnp.where(
            row == 1,
            from_resid[3 * n : 3 * n + 1],
            jnp.where(row == 2, gain_grad, jnp.where(row == 3, from_normed[6 * n : 6 * n + 1], 0.0)),
        )
        for k in range(WIDTH_STEP // LANES):
            at_row = n * blocks + at // LANES + k
            flat_ref[pl.ds(at_row, SUBLANES, stride=blocks), :] = layer[
                :, k * LANES : (k + 1) * LANES
            ]
    mean_sum = jnp.sum(mean_sum, axis=1, keepdims=True) / width
    slope = jnp.sum(slope_sum, axis=1, keepdims=True) / width * unit
    for k in range(blocks):
        columns = slice(k * LANES, (k + 1) * LANES)
        centered = table_ref[0:n, columns].astype(jnp.float32) * SHRINK - mean
        result = total_ref[:, columns] - mean_sum - centered * SHRINK**-1 * slope
        for tile in range(n // SUBLANES):
            rows = slice(tile * SUBLANES, (tile + 1) * SUBLANES)
            flat_ref[pl.ds(tile * SUBLANES * blocks + k, SUBLANES, stride=blocks), :] = result[rows]

    layer_row = (n + 1) * blocks

    def write(out_ref, core):
        for owner in range(OWNERS):
            for tile in range(PIECE * QUARTERS // SUBLANES):
                quarter, inner = divmod(tile, PIECE // SUBLANES)
                if quarter % 2 != core:
                    continue
                if tile == 0:
                    start = layer_row + owner * 15 // 2
                else:
                    start = owner * 165 // 2 + (tile - 1) * SUBLANES
                out_ref[quarter // 2 * OWNERS + owner, pl.ds(inner * SUBLANES, SUBLANES), :] = (
                    flat_ref[pl.ds(start, SUBLANES), :]
                )

    core = lax.axis_index("core")
    for value in range(2):

        @pl.when(core == value)
        def _():
            write(kept_ref, value)
            write(given_ref, 1 - value)


def local_sums(lengths, ids, masked, table, gain, resid, normed):
    width = table.shape[1]
    vmem = pl.BlockSpec(memory_space=pltpu.VMEM)
    hbm = pl.BlockSpec(memory_space=pltpu.HBM)
    out = jax.ShapeDtypeStruct((2 * OWNERS, PIECE, LANES), jnp.float32)
    return pl.pallas_call(
        sums_kernel,
        out_shape=(out, out),
        in_specs=[hbm] * 7,
        out_specs=(vmem, vmem),
        scratch_shapes=[
            pltpu.SMEM(lengths.shape, jnp.int32),
            pltpu.VMEM((1, ids.shape[0]), jnp.int32),
            pltpu.VMEM((1, ids.shape[0]), jnp.int32),
            pltpu.VMEM(table.shape, table.dtype),
            pltpu.VMEM((1, width), jnp.float32),
            pltpu.VMEM(resid.shape, resid.dtype),
            pltpu.VMEM(normed.shape, normed.dtype),
            pltpu.VMEM((VOCAB_USED, width), jnp.float32),
            pltpu.VMEM(((VOCAB_USED + SUBLANES) * width // LANES, LANES), jnp.float32),
            pltpu.SemaphoreType.DMA((5,)),
            pltpu.SemaphoreType.DMA((width // COPY_STEP,)),
            pltpu.SemaphoreType.DMA((width // COPY_STEP,)),
        ],
        compiler_params=pltpu.CompilerParams(vmem_limit_bytes=60 * 1024 * 1024),
        name="local_sums",
    )(lengths, ids[None], masked[None], table, gain[None], resid, normed)


def own_kernel(pieces_ref, layer_ref, embed_ref):
    half = LANES // 2
    odd = (lax.axis_index("y") & 1) == 1
    tiles = [
        pieces_ref[tile * SUBLANES // PIECE, pl.ds(tile * SUBLANES % PIECE, SUBLANES), :]
        for tile in range(PIECE * QUARTERS // SUBLANES)
    ]
    rolled = [pltpu.roll(tile, half, 1) for tile in tiles]
    lane = lax.broadcasted_iota(jnp.int32, (SUBLANES, LANES), 1)
    row = lax.broadcasted_iota(jnp.int32, (SUBLANES, LANES), 0)
    pieces = []
    for at, tile in enumerate(tiles):
        after = rolled[min(at + 1, len(tiles) - 1)]
        below = jnp.where(row == SUBLANES - 1, after[0:1], pltpu.roll(rolled[at], SUBLANES - 1, 0))
        pieces.append(jnp.where(odd, jnp.where(lane < half, rolled[at], below), tile))
    size = SUBLANES * LANES
    layer_ref[...] = pieces[0].reshape(size)[: layer_ref.shape[0]]
    for at, piece in enumerate(pieces[1:]):
        count = min(size, embed_ref.shape[0] - at * size)
        embed_ref[pl.ds(at * size, count)] = piece.reshape(size)[:count]


def own_blocks(pieces, layer, embed):
    vmem = pl.BlockSpec(memory_space=pltpu.VMEM)
    return pl.pallas_call(
        own_kernel,
        out_shape=(
            jax.ShapeDtypeStruct((layer,), jnp.float32),
            jax.ShapeDtypeStruct((embed,), jnp.float32),
        ),
        in_specs=[vmem],
        out_specs=(vmem, vmem),
        compiler_params=pltpu.CompilerParams(vmem_limit_bytes=4 * 1024 * 1024),
        name="own_blocks",
    )(pieces)


def to_all(block, axes, count):
    sent = jnp.broadcast_to(block[None], (count, *block.shape))
    return lax.all_to_all(sent, axes, 0, 0, tiled=True)


def on_device(lengths, ids, masked, table, gain, resid, normed):
    given, kept = local_sums(lengths, ids, masked, table, gain, resid, normed)
    pair = kept + lax.ppermute(given, "core", [(0, 1), (1, 0)])
    piece = jnp.sum(lax.all_to_all(pair, ("xh", "xl", "y"), 0, 0, tiled=True), axis=0)
    piece = jnp.sum(to_all(piece, "z", 12), axis=0)
    pieces = to_all(piece, ("xh", "core"), QUARTERS)
    return own_blocks(
        pieces, 3 * table.shape[1] // OWNERS, table.shape[0] * table.shape[1] // OWNERS
    )


def solution(mesh):
    fine = Mesh(mesh.devices.reshape(12, 2, 2, 2, 8), HOLDERS)
    in_specs = (
        P(HOLDERS, None),
        P(HOLDERS),
        P(HOLDERS),
        P(),
        P(),
        P(HOLDERS, None),
        P(HOLDERS, None),
    )
    owners = P(("xl", "y"))
    return jax.shard_map(
        on_device, mesh=fine, in_specs=in_specs, out_specs=(owners, owners), check_vma=False
    )
```

```python
import jax
import jax.numpy as jnp
from jax import lax
from jax.experimental import pallas as pl
from jax.experimental.pallas import tpu as pltpu
from jax.sharding import Mesh
from jax.sharding import PartitionSpec as P

LANES = 128
SUBLANES = 8
EPS = 1e-05
SHRINK = 2.0**-8
WIDTH_STEP = 512
COPY_STEP = 1024
VOCAB_USED = 32
OWNERS = 16
QUARTERS = 4
PIECE = 24
HOLDERS = ("z", "xh", "core", "xl", "y")


def token_rows(lengths_ref, masked_ref):
    masked = masked_ref[...].astype(jnp.float32)
    position = lax.broadcasted_iota(jnp.int32, masked.shape, 1)
    first, second = lengths_ref[0, 0], lengths_ref[0, 1]
    members = (position < first, (position >= first) & (position < first + second))
    scale = jnp.zeros_like(masked)
    for member, length in zip(members, (first, second)):
        length_f = jnp.full((1, 1), length, jnp.int32).astype(jnp.float32)
        count = jnp.sum(jnp.where(member, masked, 0.0), axis=1, keepdims=True)
        factor = 0.88 / jnp.maximum(1.0 - count / length_f, 0.5)
        scale = jnp.where(member, factor, scale)
    live = jnp.where(members[0] | members[1], 1.0, 0.0)
    return live, live * (1.0 - masked) * scale


def split3(value):
    high = value.astype(jnp.bfloat16)
    rest = value - high.astype(jnp.float32)
    mid = rest.astype(jnp.bfloat16)
    low = (rest - mid.astype(jnp.float32)).astype(jnp.bfloat16)
    return [high, mid, low]


def sum3(parts, at):
    n = VOCAB_USED
    return parts[at : at + n] + parts[at + n : at + 2 * n] + parts[at + 2 * n : at + 3 * n]


def lane_fold(value):
    total = value[:, :LANES]
    for at in range(LANES, value.shape[1], LANES):
        total = total + value[:, at : at + LANES]
    return total


def sums_kernel(
    lengths_hbm, ids_hbm, masked_hbm, table_hbm, gain_hbm, resid_hbm, normed_hbm,
    given_ref, kept_ref,
    lengths_ref, ids_ref, masked_ref, table_ref, gain_ref, resid_ref, normed_ref,
    total_ref, flat_ref, small_sem, resid_sem, normed_sem,
):
    small_copies = [
        pltpu.make_async_copy(source, target, small_sem.at[i])
        for i, (source, target) in enumerate(
            (
                (table_hbm, table_ref),
                (lengths_hbm, lengths_ref),
                (masked_hbm, masked_ref),
                (ids_hbm, ids_ref),
                (gain_hbm, gain_ref),
            )
        )
    ]
    large_copies = []
    for i in range(table_ref.shape[1] // COPY_STEP):
        columns = pl.ds(i * COPY_STEP, COPY_STEP)
        large_copies.append(
            [
                pltpu.make_async_copy(source.at[:, columns], target.at[:, columns], sem.at[i])
                for source, target, sem in (
                    (resid_hbm, resid_ref, resid_sem),
                    (normed_hbm, normed_ref, normed_sem),
                )
            ]
        )
    for copy in small_copies + sum(large_copies, []):
        copy.start()
    for copy in small_copies:
        copy.wait()
    width = table_ref.shape[1]
    blocks = width // LANES
    live, weight = token_rows(lengths_ref, masked_ref)
    n, slots = VOCAB_USED, weight.shape[1]
    small = table_ref[0:n, :].astype(jnp.float32) * SHRINK
    mean = jnp.sum(small, axis=1, keepdims=True) / width
    small = small - mean
    spread = jnp.sum(small * small, axis=1, keepdims=True) / width
    variance = jnp.minimum(spread * SHRINK**-2, 1e38)
    unit = lax.rsqrt(variance + EPS)
    unscaled = (variance + EPS) * unit

    hit = ids_ref[...] == lax.broadcasted_iota(jnp.int32, (n, slots), 0)
    weighted = jnp.where(hit, weight, 0.0)
    through = weighted * lax.rsqrt(weight * weight * variance + EPS)
    ratio = through * unscaled
    row = lax.broadcasted_iota(jnp.int32, (16, slots), 0)
    alive = jnp.where(row == 0, live, 0.0).astype(jnp.bfloat16)
    left_resid = jnp.concatenate([*split3(weighted), alive], axis=0)
    left_normed = jnp.concatenate(
        [*split3(through), *split3(through * ratio * ratio), alive], axis=0
    )

    mean_sum = jnp.zeros((n, LANES), jnp.float32)
    slope_sum = jnp.zeros((n, LANES), jnp.float32)
    for at in range(0, width, WIDTH_STEP):
        if at % COPY_STEP == 0:
            for copy in large_copies[at // COPY_STEP]:
                copy.wait()
        columns = slice(at, at + WIDTH_STEP)
        from_resid = jnp.dot(left_resid, resid_ref[:, columns], preferred_element_type=jnp.float32)
        from_normed = jnp.dot(
            left_normed, normed_ref[:, columns], preferred_element_type=jnp.float32
        )
        gain = gain_ref[:, columns]
        centered = table_ref[0:n, columns].astype(jnp.float32) * SHRINK - mean
        centered = centered * SHRINK**-1
        passed = sum3(from_normed, 0)
        gained = passed * gain
        mean_sum += lane_fold(gained)
        slope_sum += lane_fold(centered * unit * gain * sum3(from_normed, 3 * n))
        total_ref[:, columns] = sum3(from_resid, 0) + gained
        gain_grad = jnp.sum(centered * passed, axis=0, keepdims=True)
        row = lax.broadcasted_iota(jnp.int32, (SUBLANES, WIDTH_STEP), 0)
        layer = jnp.where(
            row == 1,
            from_resid[3 * n : 3 * n + 1],
            jnp.where(row == 2, gain_grad, jnp.where(row == 3, from_normed[6 * n : 6 * n + 1], 0.0)),
        )
        for k in range(WIDTH_STEP // LANES):
            at_row = n * blocks + at // LANES + k
            flat_ref[pl.ds(at_row, SUBLANES, stride=blocks), :] = layer[
                :, k * LANES : (k + 1) * LANES
            ]
    mean_sum = jnp.sum(mean_sum, axis=1, keepdims=True) / width
    slope = jnp.sum(slope_sum, axis=1, keepdims=True) / width * unit
    for k in range(blocks):
        columns = slice(k * LANES, (k + 1) * LANES)
        centered = table_ref[0:n, columns].astype(jnp.float32) * SHRINK - mean
        result = total_ref[:, columns] - mean_sum - centered * SHRINK**-1 * slope
        for tile in range(n // SUBLANES):
            rows = slice(tile * SUBLANES, (tile + 1) * SUBLANES)
            flat_ref[pl.ds(tile * SUBLANES * blocks + k, SUBLANES, stride=blocks), :] = result[rows]

    layer_row = (n + 1) * blocks

    def write(out_ref, core):
        for owner in range(OWNERS):
            for tile in range(PIECE * QUARTERS // SUBLANES):
                quarter, inner = divmod(tile, PIECE // SUBLANES)
                if quarter % 2 != core:
                    continue
                if tile == 0:
                    start = layer_row + owner * 15 // 2
                else:
                    start = owner * 165 // 2 + (tile - 1) * SUBLANES
                out_ref[quarter // 2 * OWNERS + owner, pl.ds(inner * SUBLANES, SUBLANES), :] = (
                    flat_ref[pl.ds(start, SUBLANES), :]
                )

    core = lax.axis_index("core")
    for value in range(2):

        @pl.when(core == value)
        def _():
            write(kept_ref, value)
            write(given_ref, 1 - value)


def local_sums(lengths, ids, masked, table, gain, resid, normed):
    width = table.shape[1]
    operands = (lengths, ids[None], masked[None], table, gain[None], resid, normed)
    vmem = pl.BlockSpec(memory_space=pltpu.VMEM)
    hbm = pl.BlockSpec(memory_space=pltpu.HBM)
    out = pltpu.VMEM((2 * OWNERS, PIECE, LANES), jnp.float32)
    return pl.pallas_call(
        sums_kernel,
        out_shape=(out, out),
        in_specs=[hbm] * 7,
        out_specs=(vmem, vmem),
        scratch_shapes=[
            pltpu.SMEM(lengths.shape, jnp.int32),
            pltpu.VMEM((1, ids.shape[0]), jnp.int32),
            pltpu.VMEM((1, ids.shape[0]), jnp.int32),
            pltpu.VMEM(table.shape, table.dtype),
            pltpu.VMEM((1, width), jnp.float32),
            pltpu.VMEM(resid.shape, resid.dtype),
            pltpu.VMEM(normed.shape, normed.dtype),
            pltpu.VMEM((VOCAB_USED, width), jnp.float32),
            pltpu.VMEM(((VOCAB_USED + SUBLANES) * width // LANES, LANES), jnp.float32),
            pltpu.SemaphoreType.DMA((5,)),
            pltpu.SemaphoreType.DMA((width // COPY_STEP,)),
            pltpu.SemaphoreType.DMA((width // COPY_STEP,)),
        ],
        compiler_params=pltpu.CompilerParams(vmem_limit_bytes=32 * 1024 * 1024),
        name="local_sums",
    )(*(pltpu.with_memory_space_constraint(operand, pltpu.HBM) for operand in operands))


def own_kernel(pieces_ref, layer_ref, embed_ref):
    half = LANES // 2
    odd = (lax.axis_index("y") & 1) == 1
    tiles = [
        pieces_ref[tile * SUBLANES // PIECE, pl.ds(tile * SUBLANES % PIECE, SUBLANES), :]
        for tile in range(PIECE * QUARTERS // SUBLANES)
    ]
    rolled = [pltpu.roll(tile, half, 1) for tile in tiles]
    lane = lax.broadcasted_iota(jnp.int32, (SUBLANES, LANES), 1)
    row = lax.broadcasted_iota(jnp.int32, (SUBLANES, LANES), 0)
    pieces = []
    for at, tile in enumerate(tiles):
        after = rolled[min(at + 1, len(tiles) - 1)]
        below = jnp.where(row == SUBLANES - 1, after[0:1], pltpu.roll(rolled[at], SUBLANES - 1, 0))
        pieces.append(jnp.where(odd, jnp.where(lane < half, rolled[at], below), tile))
    size = SUBLANES * LANES
    layer_ref[...] = pieces[0].reshape(size)[: layer_ref.shape[0]]
    for at, piece in enumerate(pieces[1:]):
        count = min(size, embed_ref.shape[0] - at * size)
        embed_ref[pl.ds(at * size, count)] = piece.reshape(size)[:count]


def own_blocks(pieces, layer, embed):
    vmem = pl.BlockSpec(memory_space=pltpu.VMEM)
    return pl.pallas_call(
        own_kernel,
        out_shape=(
            jax.ShapeDtypeStruct((layer,), jnp.float32),
            jax.ShapeDtypeStruct((embed,), jnp.float32),
        ),
        in_specs=[vmem],
        out_specs=(vmem, vmem),
        compiler_params=pltpu.CompilerParams(vmem_limit_bytes=4 * 1024 * 1024),
        name="own_blocks",
    )(pieces)


def to_all(block, axes, count):
    sent = jnp.broadcast_to(block[None], (count, *block.shape))
    return lax.all_to_all(sent, axes, 0, 0, tiled=True)


def on_device(lengths, ids, masked, table, gain, resid, normed):
    given, kept = local_sums(lengths, ids, masked, table, gain, resid, normed)
    pair = kept + lax.ppermute(given, "core", [(0, 1), (1, 0)])
    piece = jnp.sum(lax.all_to_all(pair, ("xh", "xl", "y"), 0, 0, tiled=True), axis=0)
    piece = jnp.sum(to_all(piece, "z", 12), axis=0)
    pieces = to_all(piece, ("xh", "core"), QUARTERS)
    return own_blocks(
        pieces, 3 * table.shape[1] // OWNERS, table.shape[0] * table.shape[1] // OWNERS
    )


def solution(mesh):
    fine = Mesh(mesh.devices.reshape(12, 2, 2, 2, 8), HOLDERS)
    in_specs = (
        P(HOLDERS, None),
        P(HOLDERS),
        P(HOLDERS),
        P(),
        P(),
        P(HOLDERS, None),
        P(HOLDERS, None),
    )
    owners = P(("xl", "y"))
    return jax.shard_map(
        on_device, mesh=fine, in_specs=in_specs, out_specs=(owners, owners), check_vma=False
    )
```

```python
import jax
import jax.numpy as jnp
from jax import lax
from jax.experimental import pallas as pl
from jax.experimental.pallas import tpu as pltpu
from jax.sharding import Mesh
from jax.sharding import PartitionSpec as P

LANES = 128
SUBLANES = 8
EPS = 1e-05
SHRINK = 2.0**-8
WIDTH_STEP = 512
COPY_STEP = 2560
VOCAB_USED = 32
OWNERS = 16
QUARTERS = 4
PIECE = 24
HOLDERS = ("z", "xh", "core", "xl", "y")


def token_rows(lengths_ref, masked_ref):
    masked = masked_ref[...].astype(jnp.float32)
    position = lax.broadcasted_iota(jnp.int32, masked.shape, 1)
    first, second = lengths_ref[0, 0], lengths_ref[0, 1]
    members = (position < first, (position >= first) & (position < first + second))
    scale = jnp.zeros_like(masked)
    for member, length in zip(members, (first, second)):
        length_f = jnp.full((1, 1), length, jnp.int32).astype(jnp.float32)
        count = jnp.sum(jnp.where(member, masked, 0.0), axis=1, keepdims=True)
        factor = 0.88 / jnp.maximum(1.0 - count / length_f, 0.5)
        scale = jnp.where(member, factor, scale)
    live = jnp.where(members[0] | members[1], 1.0, 0.0)
    return live, live * (1.0 - masked) * scale


def split3(value):
    high = value.astype(jnp.bfloat16)
    rest = value - high.astype(jnp.float32)
    mid = rest.astype(jnp.bfloat16)
    low = (rest - mid.astype(jnp.float32)).astype(jnp.bfloat16)
    return [high, mid, low]


def sum3(parts, at):
    n = VOCAB_USED
    return parts[at : at + n] + parts[at + n : at + 2 * n] + parts[at + 2 * n : at + 3 * n]


def lane_fold(value):
    total = value[:, :LANES]
    for at in range(LANES, value.shape[1], LANES):
        total = total + value[:, at : at + LANES]
    return total


def sums_kernel(
    lengths_hbm, ids_hbm, masked_hbm, table_hbm, gain_hbm, resid_hbm, normed_hbm,
    given_ref, kept_ref,
    lengths_ref, ids_ref, masked_ref, table_ref, gain_ref, resid_ref, normed_ref,
    total_ref, flat_ref, small_sem, resid_sem, normed_sem,
):
    small_copies = [
        pltpu.make_async_copy(source, target, small_sem.at[i])
        for i, (source, target) in enumerate(
            (
                (table_hbm, table_ref),
                (lengths_hbm, lengths_ref),
                (masked_hbm, masked_ref),
                (ids_hbm, ids_ref),
                (gain_hbm, gain_ref),
            )
        )
    ]
    large_copies = []
    for i in range(table_ref.shape[1] // COPY_STEP):
        columns = pl.ds(i * COPY_STEP, COPY_STEP)
        large_copies.append(
            [
                pltpu.make_async_copy(source.at[:, columns], target.at[:, columns], sem.at[i])
                for source, target, sem in (
                    (resid_hbm, resid_ref, resid_sem),
                    (normed_hbm, normed_ref, normed_sem),
                )
            ]
        )
    for copy in small_copies + sum(large_copies, []):
        copy.start()
    for copy in small_copies:
        copy.wait()
    width = table_ref.shape[1]
    blocks = width // LANES
    live, weight = token_rows(lengths_ref, masked_ref)
    n, slots = VOCAB_USED, weight.shape[1]
    small = table_ref[0:n, :].astype(jnp.float32) * SHRINK
    mean = jnp.sum(small, axis=1, keepdims=True) / width
    small = small - mean
    spread = jnp.sum(small * small, axis=1, keepdims=True) / width
    variance = jnp.minimum(spread * SHRINK**-2, 1e38)
    unit = lax.rsqrt(variance + EPS)
    unscaled = (variance + EPS) * unit

    hit = ids_ref[...] == lax.broadcasted_iota(jnp.int32, (n, slots), 0)
    weighted = jnp.where(hit, weight, 0.0)
    through = weighted * lax.rsqrt(weight * weight * variance + EPS)
    ratio = through * unscaled
    row = lax.broadcasted_iota(jnp.int32, (16, slots), 0)
    alive = jnp.where(row == 0, live, 0.0).astype(jnp.bfloat16)
    left_resid = jnp.concatenate([*split3(weighted), alive], axis=0)
    left_normed = jnp.concatenate(
        [*split3(through), *split3(through * ratio * ratio), alive], axis=0
    )

    mean_sum = jnp.zeros((n, LANES), jnp.float32)
    slope_sum = jnp.zeros((n, LANES), jnp.float32)
    for at in range(0, width, WIDTH_STEP):
        if at % COPY_STEP == 0:
            for copy in large_copies[at // COPY_STEP]:
                copy.wait()
        columns = slice(at, at + WIDTH_STEP)
        from_resid = jnp.dot(left_resid, resid_ref[:, columns], preferred_element_type=jnp.float32)
        from_normed = jnp.dot(
            left_normed, normed_ref[:, columns], preferred_element_type=jnp.float32
        )
        gain = gain_ref[:, columns]
        centered = table_ref[0:n, columns].astype(jnp.float32) * SHRINK - mean
        centered = centered * SHRINK**-1
        passed = sum3(from_normed, 0)
        gained = passed * gain
        mean_sum += lane_fold(gained)
        slope_sum += lane_fold(centered * unit * gain * sum3(from_normed, 3 * n))
        total_ref[:, columns] = sum3(from_resid, 0) + gained
        gain_grad = jnp.sum(centered * passed, axis=0, keepdims=True)
        row = lax.broadcasted_iota(jnp.int32, (SUBLANES, WIDTH_STEP), 0)
        layer = jnp.where(
            row == 1,
            from_resid[3 * n : 3 * n + 1],
            jnp.where(row == 2, gain_grad, jnp.where(row == 3, from_normed[6 * n : 6 * n + 1], 0.0)),
        )
        for k in range(WIDTH_STEP // LANES):
            at_row = n * blocks + at // LANES + k
            flat_ref[pl.ds(at_row, SUBLANES, stride=blocks), :] = layer[
                :, k * LANES : (k + 1) * LANES
            ]
    mean_sum = jnp.sum(mean_sum, axis=1, keepdims=True) / width
    slope = jnp.sum(slope_sum, axis=1, keepdims=True) / width * unit
    for k in range(blocks):
        columns = slice(k * LANES, (k + 1) * LANES)
        centered = table_ref[0:n, columns].astype(jnp.float32) * SHRINK - mean
        result = total_ref[:, columns] - mean_sum - centered * SHRINK**-1 * slope
        for tile in range(n // SUBLANES):
            rows = slice(tile * SUBLANES, (tile + 1) * SUBLANES)
            flat_ref[pl.ds(tile * SUBLANES * blocks + k, SUBLANES, stride=blocks), :] = result[rows]

    layer_row = (n + 1) * blocks

    def write(out_ref, core):
        for owner in range(OWNERS):
            for tile in range(PIECE * QUARTERS // SUBLANES):
                quarter, inner = divmod(tile, PIECE // SUBLANES)
                if quarter % 2 != core:
                    continue
                if tile == 0:
                    start = layer_row + owner * 15 // 2
                else:
                    start = owner * 165 // 2 + (tile - 1) * SUBLANES
                out_ref[quarter // 2 * OWNERS + owner, pl.ds(inner * SUBLANES, SUBLANES), :] = (
                    flat_ref[pl.ds(start, SUBLANES), :]
                )

    core = lax.axis_index("core")
    for value in range(2):

        @pl.when(core == value)
        def _():
            write(kept_ref, value)
            write(given_ref, 1 - value)


def local_sums(lengths, ids, masked, table, gain, resid, normed):
    width = table.shape[1]
    operands = (lengths, ids[None], masked[None], table, gain[None], resid, normed)
    vmem = pl.BlockSpec(memory_space=pltpu.VMEM)
    hbm = pl.BlockSpec(memory_space=pltpu.HBM)
    out = pltpu.VMEM((2 * OWNERS, PIECE, LANES), jnp.float32)
    return pl.pallas_call(
        sums_kernel,
        out_shape=(out, out),
        in_specs=[hbm] * 7,
        out_specs=(vmem, vmem),
        scratch_shapes=[
            pltpu.SMEM(lengths.shape, jnp.int32),
            pltpu.VMEM((1, ids.shape[0]), jnp.int32),
            pltpu.VMEM((1, ids.shape[0]), jnp.int32),
            pltpu.VMEM(table.shape, table.dtype),
            pltpu.VMEM((1, width), jnp.float32),
            pltpu.VMEM(resid.shape, resid.dtype),
            pltpu.VMEM(normed.shape, normed.dtype),
            pltpu.VMEM((VOCAB_USED, width), jnp.float32),
            pltpu.VMEM(((VOCAB_USED + SUBLANES) * width // LANES, LANES), jnp.float32),
            pltpu.SemaphoreType.DMA((5,)),
            pltpu.SemaphoreType.DMA((width // COPY_STEP,)),
            pltpu.SemaphoreType.DMA((width // COPY_STEP,)),
        ],
        compiler_params=pltpu.CompilerParams(vmem_limit_bytes=32 * 1024 * 1024),
        name="local_sums",
    )(*(pltpu.with_memory_space_constraint(operand, pltpu.HBM) for operand in operands))


def own_kernel(pieces_ref, layer_ref, embed_ref):
    half = LANES // 2
    odd = (lax.axis_index("y") & 1) == 1
    tiles = [
        pieces_ref[tile * SUBLANES // PIECE, pl.ds(tile * SUBLANES % PIECE, SUBLANES), :]
        for tile in range(PIECE * QUARTERS // SUBLANES)
    ]
    rolled = [pltpu.roll(tile, half, 1) for tile in tiles]
    lane = lax.broadcasted_iota(jnp.int32, (SUBLANES, LANES), 1)
    row = lax.broadcasted_iota(jnp.int32, (SUBLANES, LANES), 0)
    pieces = []
    for at, tile in enumerate(tiles):
        after = rolled[min(at + 1, len(tiles) - 1)]
        below = jnp.where(row == SUBLANES - 1, after[0:1], pltpu.roll(rolled[at], SUBLANES - 1, 0))
        pieces.append(jnp.where(odd, jnp.where(lane < half, rolled[at], below), tile))
    size = SUBLANES * LANES
    layer_ref[...] = pieces[0].reshape(size)[: layer_ref.shape[0]]
    for at, piece in enumerate(pieces[1:]):
        count = min(size, embed_ref.shape[0] - at * size)
        embed_ref[pl.ds(at * size, count)] = piece.reshape(size)[:count]


def own_blocks(pieces, layer, embed):
    vmem = pl.BlockSpec(memory_space=pltpu.VMEM)
    return pl.pallas_call(
        own_kernel,
        out_shape=(
            jax.ShapeDtypeStruct((layer,), jnp.float32),
            jax.ShapeDtypeStruct((embed,), jnp.float32),
        ),
        in_specs=[vmem],
        out_specs=(vmem, vmem),
        compiler_params=pltpu.CompilerParams(vmem_limit_bytes=4 * 1024 * 1024),
        name="own_blocks",
    )(pieces)


def to_all(block, axes, count):
    sent = jnp.broadcast_to(block[None], (count, *block.shape))
    return lax.all_to_all(sent, axes, 0, 0, tiled=True)


def on_device(lengths, ids, masked, table, gain, resid, normed):
    given, kept = local_sums(lengths, ids, masked, table, gain, resid, normed)
    both = lax.all_gather(given, "core")
    pair = kept + lax.dynamic_index_in_dim(both, 1 - lax.axis_index("core"), 0, False)
    piece = jnp.sum(lax.all_to_all(pair, ("xh", "xl", "y"), 0, 0, tiled=True), axis=0)
    piece = jnp.sum(to_all(piece, "z", 12), axis=0)
    pieces = lax.all_gather(piece, ("xh", "core"))
    return own_blocks(
        pieces, 3 * table.shape[1] // OWNERS, table.shape[0] * table.shape[1] // OWNERS
    )


def solution(mesh):
    fine = Mesh(mesh.devices.reshape(12, 2, 2, 2, 8), HOLDERS)
    in_specs = (
        P(HOLDERS, None),
        P(HOLDERS),
        P(HOLDERS),
        P(),
        P(),
        P(HOLDERS, None),
        P(HOLDERS, None),
    )
    owners = P(("xl", "y"))
    return jax.shard_map(
        on_device, mesh=fine, in_specs=in_specs, out_specs=(owners, owners), check_vma=False
    )
```

```python
import jax
import jax.numpy as jnp
from jax import lax
from jax.experimental import pallas as pl
from jax.experimental.pallas import tpu as pltpu
from jax.sharding import Mesh
from jax.sharding import PartitionSpec as P

LANES = 128
SUBLANES = 8
EPS = 1e-05
SHRINK = 2.0**-8
WIDTH_STEP = 512
VOCAB_USED = 32
OWNERS = 16
QUARTERS = 4
PIECE = 24
HOLDERS = ("z", "xh", "core", "xl", "y")


def token_rows(lengths_ref, masked_ref):
    masked = masked_ref[...].astype(jnp.float32)
    position = lax.broadcasted_iota(jnp.int32, masked.shape, 1)
    first, second = lengths_ref[0, 0], lengths_ref[0, 1]
    members = (position < first, (position >= first) & (position < first + second))
    scale = jnp.zeros_like(masked)
    for member, length in zip(members, (first, second)):
        length_f = jnp.full((1, 1), length, jnp.int32).astype(jnp.float32)
        count = jnp.sum(jnp.where(member, masked, 0.0), axis=1, keepdims=True)
        factor = 0.88 / jnp.maximum(1.0 - count / length_f, 0.5)
        scale = jnp.where(member, factor, scale)
    live = jnp.where(members[0] | members[1], 1.0, 0.0)
    return live, live * (1.0 - masked) * scale


def split2(value):
    high = value.astype(jnp.bfloat16)
    return [high, (value - high.astype(jnp.float32)).astype(jnp.bfloat16)]


def sum2(parts, at):
    n = VOCAB_USED
    return parts[at : at + n] + parts[at + n : at + 2 * n]


def lane_fold(value):
    total = value[:, :LANES]
    for at in range(LANES, value.shape[1], LANES):
        total = total + value[:, at : at + LANES]
    return total


def sums_kernel(
    lengths_hbm, ids_hbm, masked_hbm, table_hbm, gain_hbm, resid_hbm, normed_hbm,
    given_ref, kept_ref,
    lengths_ref, ids_ref, masked_ref, table_ref, gain_ref, resid_ref, normed_ref,
    center_ref, slope_gain_ref, total_ref, resid_row_ref, flat_ref, small_sem, resid_sem, normed_sem,
):
    small_copies = [
        pltpu.make_async_copy(source, target, small_sem.at[i])
        for i, (source, target) in enumerate(
            (
                (table_hbm, table_ref),
                (lengths_hbm, lengths_ref),
                (masked_hbm, masked_ref),
                (ids_hbm, ids_ref),
                (gain_hbm, gain_ref),
            )
        )
    ]
    resid_copy = pltpu.make_async_copy(resid_hbm, resid_ref, resid_sem)
    normed_copy = pltpu.make_async_copy(normed_hbm, normed_ref, normed_sem)
    for copy in [*small_copies, resid_copy, normed_copy]:
        copy.start()
    for copy in small_copies:
        copy.wait()
    width = table_ref.shape[1]
    blocks = width // LANES
    live, weight = token_rows(lengths_ref, masked_ref)
    n, slots = VOCAB_USED, weight.shape[1]
    small = table_ref[0:n, :].astype(jnp.float32) * SHRINK
    mean = jnp.sum(small, axis=1, keepdims=True) / width
    small = small - mean
    spread = jnp.sum(small * small, axis=1, keepdims=True) / width
    variance = jnp.minimum(spread * SHRINK**-2, 1e38)
    unit = lax.rsqrt(variance + EPS)
    unscaled = (variance + EPS) * unit
    for at in range(0, width, WIDTH_STEP):
        columns = slice(at, at + WIDTH_STEP)
        centered = (table_ref[0:n, columns].astype(jnp.float32) * SHRINK - mean) * SHRINK**-1
        center_ref[:, columns] = centered
        slope_gain_ref[:, columns] = centered * unit * gain_ref[:, columns]

    hit = ids_ref[...] == lax.broadcasted_iota(jnp.int32, (n, slots), 0)
    weighted = jnp.where(hit, weight, 0.0)
    through = weighted * lax.rsqrt(weight * weight * variance + EPS)
    ratio = through * unscaled
    row = lax.broadcasted_iota(jnp.int32, (16, slots), 0)
    alive = jnp.where(row == 0, live, 0.0).astype(jnp.bfloat16)
    left_resid = jnp.concatenate([*split2(weighted), alive], axis=0)
    left_normed = jnp.concatenate(
        [*split2(through), *split2(through * ratio * ratio), alive], axis=0
    )

    mean_sum = jnp.zeros((n, LANES), jnp.float32)
    slope_sum = jnp.zeros((n, LANES), jnp.float32)
    resid_copy.wait()
    for at in range(0, width, WIDTH_STEP):
        columns = slice(at, at + WIDTH_STEP)
        from_resid = jnp.dot(left_resid, resid_ref[:, columns], preferred_element_type=jnp.float32)
        total_ref[:, columns] = sum2(from_resid, 0)
        resid_row_ref[:, columns] = from_resid[2 * n : 2 * n + 1]
    normed_copy.wait()
    for at in range(0, width, WIDTH_STEP):
        columns = slice(at, at + WIDTH_STEP)
        from_normed = jnp.dot(
            left_normed, normed_ref[:, columns], preferred_element_type=jnp.float32
        )
        passed = sum2(from_normed, 0)
        gained = passed * gain_ref[:, columns]
        mean_sum += lane_fold(gained)
        slope_sum += lane_fold(slope_gain_ref[:, columns] * sum2(from_normed, 2 * n))
        total_ref[:, columns] += gained
        gain_grad = jnp.sum(center_ref[:, columns] * passed, axis=0, keepdims=True)
        row = lax.broadcasted_iota(jnp.int32, (SUBLANES, WIDTH_STEP), 0)
        layer = jnp.where(
            row == 1,
            resid_row_ref[:, columns],
            jnp.where(row == 2, gain_grad, jnp.where(row == 3, from_normed[4 * n : 4 * n + 1], 0.0)),
        )
        for k in range(WIDTH_STEP // LANES):
            at_row = n * blocks + at // LANES + k
            flat_ref[pl.ds(at_row, SUBLANES, stride=blocks), :] = layer[
                :, k * LANES : (k + 1) * LANES
            ]
    mean_sum = jnp.sum(mean_sum, axis=1, keepdims=True) / width
    slope = jnp.sum(slope_sum, axis=1, keepdims=True) / width * unit
    for k in range(blocks):
        columns = slice(k * LANES, (k + 1) * LANES)
        result = total_ref[:, columns] - mean_sum - center_ref[:, columns] * slope
        for tile in range(n // SUBLANES):
            rows = slice(tile * SUBLANES, (tile + 1) * SUBLANES)
            flat_ref[pl.ds(tile * SUBLANES * blocks + k, SUBLANES, stride=blocks), :] = result[rows]

    layer_row = (n + 1) * blocks

    def write(out_ref, core):
        for owner in range(OWNERS):
            for tile in range(PIECE * QUARTERS // SUBLANES):
                quarter, inner = divmod(tile, PIECE // SUBLANES)
                if quarter % 2 != core:
                    continue
                if tile == 0:
                    start = layer_row + owner * 15 // 2
                else:
                    start = owner * 165 // 2 + (tile - 1) * SUBLANES
                out_ref[quarter // 2 * OWNERS + owner, pl.ds(inner * SUBLANES, SUBLANES), :] = (
                    flat_ref[pl.ds(start, SUBLANES), :]
                )

    core = lax.axis_index("core")
    for value in range(2):

        @pl.when(core == value)
        def _():
            write(kept_ref, value)
            write(given_ref, 1 - value)


def local_sums(lengths, ids, masked, table, gain, resid, normed):
    width = table.shape[1]
    operands = (lengths, ids[None], masked[None], table, gain[None], resid, normed)
    vmem = pl.BlockSpec(memory_space=pltpu.VMEM)
    hbm = pl.BlockSpec(memory_space=pltpu.HBM)
    out = pltpu.VMEM((2 * OWNERS, PIECE, LANES), jnp.float32)
    return pl.pallas_call(
        sums_kernel,
        out_shape=(out, out),
        in_specs=[hbm] * 7,
        out_specs=(vmem, vmem),
        scratch_shapes=[
            pltpu.SMEM(lengths.shape, jnp.int32),
            pltpu.VMEM((1, ids.shape[0]), jnp.int32),
            pltpu.VMEM((1, ids.shape[0]), jnp.int32),
            pltpu.VMEM(table.shape, table.dtype),
            pltpu.VMEM((1, width), jnp.float32),
            pltpu.VMEM(resid.shape, resid.dtype),
            pltpu.VMEM(normed.shape, normed.dtype),
            pltpu.VMEM((VOCAB_USED, width), jnp.float32),
            pltpu.VMEM((VOCAB_USED, width), jnp.float32),
            pltpu.VMEM((VOCAB_USED, width), jnp.float32),
            pltpu.VMEM((1, width), jnp.float32),
            pltpu.VMEM(((VOCAB_USED + SUBLANES) * width // LANES, LANES), jnp.float32),
            pltpu.SemaphoreType.DMA((5,)),
            pltpu.SemaphoreType.DMA,
            pltpu.SemaphoreType.DMA,
        ],
        compiler_params=pltpu.CompilerParams(vmem_limit_bytes=32 * 1024 * 1024),
        name="local_sums",
    )(*(pltpu.with_memory_space_constraint(operand, pltpu.HBM) for operand in operands))


def own_kernel(pieces_ref, layer_ref, embed_ref):
    half = LANES // 2
    odd = (lax.axis_index("y") & 1) == 1
    tiles = [
        pieces_ref[tile * SUBLANES // PIECE, pl.ds(tile * SUBLANES % PIECE, SUBLANES), :]
        for tile in range(PIECE * QUARTERS // SUBLANES)
    ]
    rolled = [pltpu.roll(tile, half, 1) for tile in tiles]
    lane = lax.broadcasted_iota(jnp.int32, (SUBLANES, LANES), 1)
    row = lax.broadcasted_iota(jnp.int32, (SUBLANES, LANES), 0)
    pieces = []
    for at, tile in enumerate(tiles):
        after = rolled[min(at + 1, len(tiles) - 1)]
        below = jnp.where(row == SUBLANES - 1, after[0:1], pltpu.roll(rolled[at], SUBLANES - 1, 0))
        pieces.append(jnp.where(odd, jnp.where(lane < half, rolled[at], below), tile))
    size = SUBLANES * LANES
    layer_ref[...] = pieces[0].reshape(size)[: layer_ref.shape[0]]
    for at, piece in enumerate(pieces[1:]):
        count = min(size, embed_ref.shape[0] - at * size)
        embed_ref[pl.ds(at * size, count)] = piece.reshape(size)[:count]


def own_blocks(pieces, layer, embed):
    vmem = pl.BlockSpec(memory_space=pltpu.VMEM)
    return pl.pallas_call(
        own_kernel,
        out_shape=(
            jax.ShapeDtypeStruct((layer,), jnp.float32),
            jax.ShapeDtypeStruct((embed,), jnp.float32),
        ),
        in_specs=[vmem],
        out_specs=(vmem, vmem),
        compiler_params=pltpu.CompilerParams(vmem_limit_bytes=4 * 1024 * 1024),
        name="own_blocks",
    )(pieces)


def to_all(block, axes, count):
    sent = jnp.broadcast_to(block[None], (count, *block.shape))
    return lax.all_to_all(sent, axes, 0, 0, tiled=True)


def on_device(lengths, ids, masked, table, gain, resid, normed):
    given, kept = local_sums(lengths, ids, masked, table, gain, resid, normed)
    both = lax.all_gather(given, "core")
    pair = kept + lax.dynamic_index_in_dim(both, 1 - lax.axis_index("core"), 0, False)
    piece = jnp.sum(lax.all_to_all(pair, ("xh", "xl", "y"), 0, 0, tiled=True), axis=0)
    piece = jnp.sum(to_all(piece, "z", 12), axis=0)
    pieces = lax.all_gather(piece, ("xh", "core"))
    return own_blocks(
        pieces, 3 * table.shape[1] // OWNERS, table.shape[0] * table.shape[1] // OWNERS
    )


def solution(mesh):
    fine = Mesh(mesh.devices.reshape(12, 2, 2, 2, 8), HOLDERS)
    in_specs = (
        P(HOLDERS, None),
        P(HOLDERS),
        P(HOLDERS),
        P(),
        P(),
        P(HOLDERS, None),
        P(HOLDERS, None),
    )
    owners = P(("xl", "y"))
    return jax.shard_map(
        on_device, mesh=fine, in_specs=in_specs, out_specs=(owners, owners), check_vma=False
    )
```

```python
import jax
import jax.numpy as jnp
from jax import lax
from jax.experimental import pallas as pl
from jax.experimental.pallas import tpu as pltpu
from jax.sharding import Mesh
from jax.sharding import PartitionSpec as P

LANES = 128
SUBLANES = 8
EPS = 1e-05
SHRINK = 2.0**-8
WIDTH_STEP = 512
VOCAB_USED = 32
OWNERS = 16
QUARTERS = 4
PLANE = [x * 8 + y for x in (3, 2, 1, 0) for y in (5, 6, 4, 7, 3, 2, 1, 0)]
PLANES = [8, 7, 9, 6, 10, 5, 11, 4, 3, 2, 1, 0]
PIECE = 24
HOLDERS = ("z", "xh", "core", "xl", "y")


def token_rows(lengths_ref, masked_ref):
    masked = masked_ref[...].astype(jnp.float32)
    position = lax.broadcasted_iota(jnp.int32, masked.shape, 1)
    first, second = lengths_ref[0, 0], lengths_ref[0, 1]
    members = (position < first, (position >= first) & (position < first + second))
    scale = jnp.zeros_like(masked)
    for member, length in zip(members, (first, second)):
        length_f = jnp.full((1, 1), length, jnp.int32).astype(jnp.float32)
        count = jnp.sum(jnp.where(member, masked, 0.0), axis=1, keepdims=True)
        factor = 0.88 / jnp.maximum(1.0 - count / length_f, 0.5)
        scale = jnp.where(member, factor, scale)
    live = jnp.where(members[0] | members[1], 1.0, 0.0)
    return live, live * (1.0 - masked) * scale


def split2(value):
    high = value.astype(jnp.bfloat16)
    return [high, (value - high.astype(jnp.float32)).astype(jnp.bfloat16)]


def sum2(parts, at):
    n = VOCAB_USED
    return parts[at : at + n] + parts[at + n : at + 2 * n]


def lane_fold(value):
    total = value[:, :LANES]
    for at in range(LANES, value.shape[1], LANES):
        total = total + value[:, at : at + LANES]
    return total


def sums_kernel(
    lengths_hbm, ids_hbm, masked_hbm, table_hbm, gain_hbm, resid_hbm, normed_hbm,
    given_ref, kept_ref,
    lengths_ref, ids_ref, masked_ref, table_ref, gain_ref, resid_ref, normed_ref,
    center_ref, slope_gain_ref, total_ref, resid_row_ref, flat_ref, small_sem, resid_sem, normed_sem,
):
    small_copies = [
        pltpu.make_async_copy(source, target, small_sem.at[i])
        for i, (source, target) in enumerate(
            (
                (table_hbm, table_ref),
                (lengths_hbm, lengths_ref),
                (masked_hbm, masked_ref),
                (ids_hbm, ids_ref),
                (gain_hbm, gain_ref),
            )
        )
    ]
    resid_copy = pltpu.make_async_copy(resid_hbm, resid_ref, resid_sem)
    normed_copy = pltpu.make_async_copy(normed_hbm, normed_ref, normed_sem)
    for copy in [*small_copies, resid_copy, normed_copy]:
        copy.start()
    for copy in small_copies:
        copy.wait()
    width = table_ref.shape[1]
    blocks = width // LANES
    live, weight = token_rows(lengths_ref, masked_ref)
    n, slots = VOCAB_USED, weight.shape[1]
    small = table_ref[0:n, :].astype(jnp.float32) * SHRINK
    mean = jnp.sum(small, axis=1, keepdims=True) / width
    small = small - mean
    spread = jnp.sum(small * small, axis=1, keepdims=True) / width
    variance = jnp.minimum(spread * SHRINK**-2, 1e38)
    unit = lax.rsqrt(variance + EPS)
    unscaled = (variance + EPS) * unit
    for at in range(0, width, WIDTH_STEP):
        columns = slice(at, at + WIDTH_STEP)
        centered = (table_ref[0:n, columns].astype(jnp.float32) * SHRINK - mean) * SHRINK**-1
        center_ref[:, columns] = centered
        slope_gain_ref[:, columns] = centered * unit * gain_ref[:, columns]

    hit = ids_ref[...] == lax.broadcasted_iota(jnp.int32, (n, slots), 0)
    weighted = jnp.where(hit, weight, 0.0)
    through = weighted * lax.rsqrt(weight * weight * variance + EPS)
    ratio = through * unscaled
    row = lax.broadcasted_iota(jnp.int32, (16, slots), 0)
    alive = jnp.where(row == 0, live, 0.0).astype(jnp.bfloat16)
    left_resid = jnp.concatenate([*split2(weighted), alive], axis=0)
    left_normed = jnp.concatenate(
        [*split2(through), *split2(through * ratio * ratio), alive], axis=0
    )

    mean_sum = jnp.zeros((n, LANES), jnp.float32)
    slope_sum = jnp.zeros((n, LANES), jnp.float32)
    resid_copy.wait()
    for at in range(0, width, WIDTH_STEP):
        columns = slice(at, at + WIDTH_STEP)
        from_resid = jnp.dot(left_resid, resid_ref[:, columns], preferred_element_type=jnp.float32)
        total_ref[:, columns] = sum2(from_resid, 0)
        resid_row_ref[:, columns] = from_resid[2 * n : 2 * n + 1]
    normed_copy.wait()
    for at in range(0, width, WIDTH_STEP):
        columns = slice(at, at + WIDTH_STEP)
        from_normed = jnp.dot(
            left_normed, normed_ref[:, columns], preferred_element_type=jnp.float32
        )
        passed = sum2(from_normed, 0)
        gained = passed * gain_ref[:, columns]
        mean_sum += lane_fold(gained)
        slope_sum += lane_fold(slope_gain_ref[:, columns] * sum2(from_normed, 2 * n))
        total_ref[:, columns] += gained
        gain_grad = jnp.sum(center_ref[:, columns] * passed, axis=0, keepdims=True)
        row = lax.broadcasted_iota(jnp.int32, (SUBLANES, WIDTH_STEP), 0)
        layer = jnp.where(
            row == 1,
            resid_row_ref[:, columns],
            jnp.where(row == 2, gain_grad, jnp.where(row == 3, from_normed[4 * n : 4 * n + 1], 0.0)),
        )
        for k in range(WIDTH_STEP // LANES):
            at_row = n * blocks + at // LANES + k
            flat_ref[pl.ds(at_row, SUBLANES, stride=blocks), :] = layer[
                :, k * LANES : (k + 1) * LANES
            ]
    mean_sum = jnp.sum(mean_sum, axis=1, keepdims=True) / width
    slope = jnp.sum(slope_sum, axis=1, keepdims=True) / width * unit
    for k in range(blocks):
        columns = slice(k * LANES, (k + 1) * LANES)
        result = total_ref[:, columns] - mean_sum - center_ref[:, columns] * slope
        for tile in range(n // SUBLANES):
            rows = slice(tile * SUBLANES, (tile + 1) * SUBLANES)
            flat_ref[pl.ds(tile * SUBLANES * blocks + k, SUBLANES, stride=blocks), :] = result[rows]

    layer_row = (n + 1) * blocks

    def write(out_ref, core):
        for owner in range(OWNERS):
            for tile in range(PIECE * QUARTERS // SUBLANES):
                quarter, inner = divmod(tile, PIECE // SUBLANES)
                if quarter % 2 != core:
                    continue
                if tile == 0:
                    start = layer_row + owner * 15 // 2
                else:
                    start = owner * 165 // 2 + (tile - 1) * SUBLANES
                out_ref[PLANE.index(quarter // 2 * OWNERS + owner), pl.ds(inner * SUBLANES, SUBLANES), :] = (
                    flat_ref[pl.ds(start, SUBLANES), :]
                )

    core = lax.axis_index("core")
    for value in range(2):

        @pl.when(core == value)
        def _():
            write(kept_ref, value)
            write(given_ref, 1 - value)


def local_sums(lengths, ids, masked, table, gain, resid, normed):
    width = table.shape[1]
    operands = (lengths, ids[None], masked[None], table, gain[None], resid, normed)
    vmem = pl.BlockSpec(memory_space=pltpu.VMEM)
    hbm = pl.BlockSpec(memory_space=pltpu.HBM)
    out = pltpu.VMEM((2 * OWNERS, PIECE, LANES), jnp.float32)
    return pl.pallas_call(
        sums_kernel,
        out_shape=(out, out),
        in_specs=[hbm] * 7,
        out_specs=(vmem, vmem),
        scratch_shapes=[
            pltpu.SMEM(lengths.shape, jnp.int32),
            pltpu.VMEM((1, ids.shape[0]), jnp.int32),
            pltpu.VMEM((1, ids.shape[0]), jnp.int32),
            pltpu.VMEM(table.shape, table.dtype),
            pltpu.VMEM((1, width), jnp.float32),
            pltpu.VMEM(resid.shape, resid.dtype),
            pltpu.VMEM(normed.shape, normed.dtype),
            pltpu.VMEM((VOCAB_USED, width), jnp.float32),
            pltpu.VMEM((VOCAB_USED, width), jnp.float32),
            pltpu.VMEM((VOCAB_USED, width), jnp.float32),
            pltpu.VMEM((1, width), jnp.float32),
            pltpu.VMEM(((VOCAB_USED + SUBLANES) * width // LANES, LANES), jnp.float32),
            pltpu.SemaphoreType.DMA((5,)),
            pltpu.SemaphoreType.DMA,
            pltpu.SemaphoreType.DMA,
        ],
        compiler_params=pltpu.CompilerParams(vmem_limit_bytes=32 * 1024 * 1024),
        name="local_sums",
    )(*(pltpu.with_memory_space_constraint(operand, pltpu.HBM) for operand in operands))


def own_kernel(pieces_ref, layer_ref, embed_ref):
    half = LANES // 2
    odd = (lax.axis_index("y") & 1) == 1
    tiles = [
        pieces_ref[tile * SUBLANES // PIECE, pl.ds(tile * SUBLANES % PIECE, SUBLANES), :]
        for tile in range(PIECE * QUARTERS // SUBLANES)
    ]
    rolled = [pltpu.roll(tile, half, 1) for tile in tiles]
    lane = lax.broadcasted_iota(jnp.int32, (SUBLANES, LANES), 1)
    row = lax.broadcasted_iota(jnp.int32, (SUBLANES, LANES), 0)
    pieces = []
    for at, tile in enumerate(tiles):
        after = rolled[min(at + 1, len(tiles) - 1)]
        below = jnp.where(row == SUBLANES - 1, after[0:1], pltpu.roll(rolled[at], SUBLANES - 1, 0))
        pieces.append(jnp.where(odd, jnp.where(lane < half, rolled[at], below), tile))
    size = SUBLANES * LANES
    layer_ref[...] = pieces[0].reshape(size)[: layer_ref.shape[0]]
    for at, piece in enumerate(pieces[1:]):
        count = min(size, embed_ref.shape[0] - at * size)
        embed_ref[pl.ds(at * size, count)] = piece.reshape(size)[:count]


def own_blocks(pieces, layer, embed):
    vmem = pl.BlockSpec(memory_space=pltpu.VMEM)
    return pl.pallas_call(
        own_kernel,
        out_shape=(
            jax.ShapeDtypeStruct((layer,), jnp.float32),
            jax.ShapeDtypeStruct((embed,), jnp.float32),
        ),
        in_specs=[vmem],
        out_specs=(vmem, vmem),
        compiler_params=pltpu.CompilerParams(vmem_limit_bytes=4 * 1024 * 1024),
        name="own_blocks",
    )(pieces)


def to_all(block, axes, order):
    sent = jnp.broadcast_to(block[None], (len(order), *block.shape))
    return lax.all_to_all(sent, axes, 0, 0, axis_index_groups=[order], tiled=True)


def on_device(lengths, ids, masked, table, gain, resid, normed):
    given, kept = local_sums(lengths, ids, masked, table, gain, resid, normed)
    both = lax.all_gather(given, "core")
    pair = kept + lax.dynamic_index_in_dim(both, 1 - lax.axis_index("core"), 0, False)
    piece = jnp.sum(lax.all_to_all(pair, ("xh", "xl", "y"), 0, 0, axis_index_groups=[PLANE], tiled=True), axis=0)
    piece = jnp.sum(to_all(piece, "z", PLANES), axis=0)
    pieces = lax.all_gather(piece, ("xh", "core"))
    return own_blocks(
        pieces, 3 * table.shape[1] // OWNERS, table.shape[0] * table.shape[1] // OWNERS
    )


def solution(mesh):
    fine = Mesh(mesh.devices.reshape(12, 2, 2, 2, 8), HOLDERS)
    in_specs = (
        P(HOLDERS, None),
        P(HOLDERS),
        P(HOLDERS),
        P(),
        P(),
        P(HOLDERS, None),
        P(HOLDERS, None),
    )
    owners = P(("xl", "y"))
    return jax.shard_map(
        on_device, mesh=fine, in_specs=in_specs, out_specs=(owners, owners), check_vma=False
    )
```

```python
import jax
import jax.numpy as jnp
from jax import lax
from jax.experimental import pallas as pl
from jax.experimental.pallas import tpu as pltpu
from jax.sharding import Mesh
from jax.sharding import PartitionSpec as P

LANES = 128
SUBLANES = 8
EPS = 1e-05
SHRINK = 2.0**-8
WIDTH_STEP = 512
VOCAB_USED = 32
OWNERS = 16
QUARTERS = 4
PLANE = [x * 8 + y for y in (5, 6, 4, 7, 3, 2, 1, 0) for x in (3, 2, 1, 0)]
PLANES = [8, 7, 9, 6, 10, 5, 11, 4, 3, 2, 1, 0]
PIECE = 24
HOLDERS = ("z", "xh", "core", "xl", "y")


def token_rows(lengths_ref, masked_ref):
    masked = masked_ref[...].astype(jnp.float32)
    position = lax.broadcasted_iota(jnp.int32, masked.shape, 1)
    first, second = lengths_ref[0, 0], lengths_ref[0, 1]
    members = (position < first, (position >= first) & (position < first + second))
    scale = jnp.zeros_like(masked)
    for member, length in zip(members, (first, second)):
        length_f = jnp.full((1, 1), length, jnp.int32).astype(jnp.float32)
        count = jnp.sum(jnp.where(member, masked, 0.0), axis=1, keepdims=True)
        factor = 0.88 / jnp.maximum(1.0 - count / length_f, 0.5)
        scale = jnp.where(member, factor, scale)
    live = jnp.where(members[0] | members[1], 1.0, 0.0)
    return live, live * (1.0 - masked) * scale


def split2(value):
    high = value.astype(jnp.bfloat16)
    return [high, (value - high.astype(jnp.float32)).astype(jnp.bfloat16)]


def sum2(parts, at):
    n = VOCAB_USED
    return parts[at : at + n] + parts[at + n : at + 2 * n]


def lane_fold(value):
    total = value[:, :LANES]
    for at in range(LANES, value.shape[1], LANES):
        total = total + value[:, at : at + LANES]
    return total


def sums_kernel(
    lengths_hbm, ids_hbm, masked_hbm, table_hbm, gain_hbm, resid_hbm, normed_hbm,
    given_ref, kept_ref,
    lengths_ref, ids_ref, masked_ref, table_ref, gain_ref, resid_ref, normed_ref,
    center_ref, slope_gain_ref, total_ref, resid_row_ref, flat_ref, small_sem, resid_sem, normed_sem,
):
    small_copies = [
        pltpu.make_async_copy(source, target, small_sem.at[i])
        for i, (source, target) in enumerate(
            (
                (table_hbm, table_ref),
                (lengths_hbm, lengths_ref),
                (masked_hbm, masked_ref),
                (ids_hbm, ids_ref),
                (gain_hbm, gain_ref),
            )
        )
    ]
    resid_copy = pltpu.make_async_copy(resid_hbm, resid_ref, resid_sem)
    normed_copy = pltpu.make_async_copy(normed_hbm, normed_ref, normed_sem)
    for copy in [*small_copies, resid_copy, normed_copy]:
        copy.start()
    for copy in small_copies:
        copy.wait()
    width = table_ref.shape[1]
    blocks = width // LANES
    live, weight = token_rows(lengths_ref, masked_ref)
    n, slots = VOCAB_USED, weight.shape[1]
    small = table_ref[0:n, :].astype(jnp.float32) * SHRINK
    mean = jnp.sum(small, axis=1, keepdims=True) / width
    small = small - mean
    spread = jnp.sum(small * small, axis=1, keepdims=True) / width
    variance = jnp.minimum(spread * SHRINK**-2, 1e38)
    unit = lax.rsqrt(variance + EPS)
    unscaled = (variance + EPS) * unit
    for at in range(0, width, WIDTH_STEP):
        columns = slice(at, at + WIDTH_STEP)
        centered = (table_ref[0:n, columns].astype(jnp.float32) * SHRINK - mean) * SHRINK**-1
        center_ref[:, columns] = centered
        slope_gain_ref[:, columns] = centered * unit * gain_ref[:, columns]

    hit = ids_ref[...] == lax.broadcasted_iota(jnp.int32, (n, slots), 0)
    weighted = jnp.where(hit, weight, 0.0)
    through = weighted * lax.rsqrt(weight * weight * variance + EPS)
    ratio = through * unscaled
    row = lax.broadcasted_iota(jnp.int32, (16, slots), 0)
    alive = jnp.where(row == 0, live, 0.0).astype(jnp.bfloat16)
    left_resid = jnp.concatenate([*split2(weighted), alive], axis=0)
    left_normed = jnp.concatenate(
        [*split2(through), *split2(through * ratio * ratio), alive], axis=0
    )

    mean_sum = jnp.zeros((n, LANES), jnp.float32)
    slope_sum = jnp.zeros((n, LANES), jnp.float32)
    resid_copy.wait()
    for at in range(0, width, WIDTH_STEP):
        columns = slice(at, at + WIDTH_STEP)
        from_resid = jnp.dot(left_resid, resid_ref[:, columns], preferred_element_type=jnp.float32)
        total_ref[:, columns] = sum2(from_resid, 0)
        resid_row_ref[:, columns] = from_resid[2 * n : 2 * n + 1]
    normed_copy.wait()
    for at in range(0, width, WIDTH_STEP):
        columns = slice(at, at + WIDTH_STEP)
        from_normed = jnp.dot(
            left_normed, normed_ref[:, columns], preferred_element_type=jnp.float32
        )
        passed = sum2(from_normed, 0)
        gained = passed * gain_ref[:, columns]
        mean_sum += lane_fold(gained)
        slope_sum += lane_fold(slope_gain_ref[:, columns] * sum2(from_normed, 2 * n))
        total_ref[:, columns] += gained
        gain_grad = jnp.sum(center_ref[:, columns] * passed, axis=0, keepdims=True)
        row = lax.broadcasted_iota(jnp.int32, (SUBLANES, WIDTH_STEP), 0)
        layer = jnp.where(
            row == 1,
            resid_row_ref[:, columns],
            jnp.where(row == 2, gain_grad, jnp.where(row == 3, from_normed[4 * n : 4 * n + 1], 0.0)),
        )
        for k in range(WIDTH_STEP // LANES):
            at_row = n * blocks + at // LANES + k
            flat_ref[pl.ds(at_row, SUBLANES, stride=blocks), :] = layer[
                :, k * LANES : (k + 1) * LANES
            ]
    mean_sum = jnp.sum(mean_sum, axis=1, keepdims=True) / width
    slope = jnp.sum(slope_sum, axis=1, keepdims=True) / width * unit
    for k in range(blocks):
        columns = slice(k * LANES, (k + 1) * LANES)
        result = total_ref[:, columns] - mean_sum - center_ref[:, columns] * slope
        for tile in range(n // SUBLANES):
            rows = slice(tile * SUBLANES, (tile + 1) * SUBLANES)
            flat_ref[pl.ds(tile * SUBLANES * blocks + k, SUBLANES, stride=blocks), :] = result[rows]

    layer_row = (n + 1) * blocks

    def write(out_ref, core):
        for owner in range(OWNERS):
            for tile in range(PIECE * QUARTERS // SUBLANES):
                quarter, inner = divmod(tile, PIECE // SUBLANES)
                if quarter % 2 != core:
                    continue
                if tile == 0:
                    start = layer_row + owner * 15 // 2
                else:
                    start = owner * 165 // 2 + (tile - 1) * SUBLANES
                out_ref[PLANE.index(quarter // 2 * OWNERS + owner), pl.ds(inner * SUBLANES, SUBLANES), :] = (
                    flat_ref[pl.ds(start, SUBLANES), :]
                )

    core = lax.axis_index("core")
    for value in range(2):

        @pl.when(core == value)
        def _():
            write(kept_ref, value)
            write(given_ref, 1 - value)


def local_sums(lengths, ids, masked, table, gain, resid, normed):
    width = table.shape[1]
    operands = (lengths, ids[None], masked[None], table, gain[None], resid, normed)
    vmem = pl.BlockSpec(memory_space=pltpu.VMEM)
    hbm = pl.BlockSpec(memory_space=pltpu.HBM)
    out = pltpu.VMEM((2 * OWNERS, PIECE, LANES), jnp.float32)
    return pl.pallas_call(
        sums_kernel,
        out_shape=(out, out),
        in_specs=[hbm] * 7,
        out_specs=(vmem, vmem),
        scratch_shapes=[
            pltpu.SMEM(lengths.shape, jnp.int32),
            pltpu.VMEM((1, ids.shape[0]), jnp.int32),
            pltpu.VMEM((1, ids.shape[0]), jnp.int32),
            pltpu.VMEM(table.shape, table.dtype),
            pltpu.VMEM((1, width), jnp.float32),
            pltpu.VMEM(resid.shape, resid.dtype),
            pltpu.VMEM(normed.shape, normed.dtype),
            pltpu.VMEM((VOCAB_USED, width), jnp.float32),
            pltpu.VMEM((VOCAB_USED, width), jnp.float32),
            pltpu.VMEM((VOCAB_USED, width), jnp.float32),
            pltpu.VMEM((1, width), jnp.float32),
            pltpu.VMEM(((VOCAB_USED + SUBLANES) * width // LANES, LANES), jnp.float32),
            pltpu.SemaphoreType.DMA((5,)),
            pltpu.SemaphoreType.DMA,
            pltpu.SemaphoreType.DMA,
        ],
        compiler_params=pltpu.CompilerParams(vmem_limit_bytes=32 * 1024 * 1024),
        name="local_sums",
    )(*(pltpu.with_memory_space_constraint(operand, pltpu.HBM) for operand in operands))


def own_kernel(pieces_ref, layer_ref, embed_ref):
    half = LANES // 2
    odd = (lax.axis_index("y") & 1) == 1
    tiles = [
        pieces_ref[tile * SUBLANES // PIECE, pl.ds(tile * SUBLANES % PIECE, SUBLANES), :]
        for tile in range(PIECE * QUARTERS // SUBLANES)
    ]
    rolled = [pltpu.roll(tile, half, 1) for tile in tiles]
    lane = lax.broadcasted_iota(jnp.int32, (SUBLANES, LANES), 1)
    row = lax.broadcasted_iota(jnp.int32, (SUBLANES, LANES), 0)
    pieces = []
    for at, tile in enumerate(tiles):
        after = rolled[min(at + 1, len(tiles) - 1)]
        below = jnp.where(row == SUBLANES - 1, after[0:1], pltpu.roll(rolled[at], SUBLANES - 1, 0))
        pieces.append(jnp.where(odd, jnp.where(lane < half, rolled[at], below), tile))
    size = SUBLANES * LANES
    layer_ref[...] = pieces[0].reshape(size)[: layer_ref.shape[0]]
    for at, piece in enumerate(pieces[1:]):
        count = min(size, embed_ref.shape[0] - at * size)
        embed_ref[pl.ds(at * size, count)] = piece.reshape(size)[:count]


def own_blocks(pieces, layer, embed):
    vmem = pl.BlockSpec(memory_space=pltpu.VMEM)
    return pl.pallas_call(
        own_kernel,
        out_shape=(
            jax.ShapeDtypeStruct((layer,), jnp.float32),
            jax.ShapeDtypeStruct((embed,), jnp.float32),
        ),
        in_specs=[vmem],
        out_specs=(vmem, vmem),
        compiler_params=pltpu.CompilerParams(vmem_limit_bytes=4 * 1024 * 1024),
        name="own_blocks",
    )(pieces)


def to_all(block, axes, order):
    sent = jnp.broadcast_to(block[None], (len(order), *block.shape))
    return lax.all_to_all(sent, axes, 0, 0, axis_index_groups=[order], tiled=True)


def on_device(lengths, ids, masked, table, gain, resid, normed):
    given, kept = local_sums(lengths, ids, masked, table, gain, resid, normed)
    both = lax.all_gather(given, "core")
    pair = kept + lax.dynamic_index_in_dim(both, 1 - lax.axis_index("core"), 0, False)
    piece = jnp.sum(lax.all_to_all(pair, ("xh", "xl", "y"), 0, 0, axis_index_groups=[PLANE], tiled=True), axis=0)
    piece = jnp.sum(to_all(piece, "z", PLANES), axis=0)
    pieces = lax.all_gather(piece, ("xh", "core"))
    return own_blocks(
        pieces, 3 * table.shape[1] // OWNERS, table.shape[0] * table.shape[1] // OWNERS
    )


def solution(mesh):
    fine = Mesh(mesh.devices.reshape(12, 2, 2, 2, 8), HOLDERS)
    in_specs = (
        P(HOLDERS, None),
        P(HOLDERS),
        P(HOLDERS),
        P(),
        P(),
        P(HOLDERS, None),
        P(HOLDERS, None),
    )
    owners = P(("xl", "y"))
    return jax.shard_map(
        on_device, mesh=fine, in_specs=in_specs, out_specs=(owners, owners), check_vma=False
    )
```

```python
import jax
import jax.numpy as jnp
from jax import lax
from jax.experimental import pallas as pl
from jax.experimental.pallas import tpu as pltpu
from jax.sharding import Mesh
from jax.sharding import PartitionSpec as P

LANES = 128
SUBLANES = 8
EPS = 1e-05
SHRINK = 2.0**-8
WIDTH_STEP = 512
VOCAB_USED = 32
OWNERS = 16
QUARTERS = 4
PLANE = [x * 8 + y for y in (5, 6, 4, 7, 3, 2, 1, 0) for x in (3, 2, 1, 0)]
PLANES = [8, 9, 7, 10, 6, 11, 5, 4, 3, 2, 1, 0]
PIECE = 24
HOLDERS = ("z", "xh", "core", "xl", "y")


def token_rows(lengths_ref, masked_ref):
    masked = masked_ref[...].astype(jnp.float32)
    position = lax.broadcasted_iota(jnp.int32, masked.shape, 1)
    first, second = lengths_ref[0, 0], lengths_ref[0, 1]
    members = (position < first, (position >= first) & (position < first + second))
    scale = jnp.zeros_like(masked)
    for member, length in zip(members, (first, second)):
        length_f = jnp.full((1, 1), length, jnp.int32).astype(jnp.float32)
        count = jnp.sum(jnp.where(member, masked, 0.0), axis=1, keepdims=True)
        factor = 0.88 / jnp.maximum(1.0 - count / length_f, 0.5)
        scale = jnp.where(member, factor, scale)
    live = jnp.where(members[0] | members[1], 1.0, 0.0)
    return live, live * (1.0 - masked) * scale


def split2(value):
    high = value.astype(jnp.bfloat16)
    return [high, (value - high.astype(jnp.float32)).astype(jnp.bfloat16)]


def sum2(parts, at):
    n = VOCAB_USED
    return parts[at : at + n] + parts[at + n : at + 2 * n]


def lane_fold(value):
    total = value[:, :LANES]
    for at in range(LANES, value.shape[1], LANES):
        total = total + value[:, at : at + LANES]
    return total


def sums_kernel(
    lengths_hbm, ids_hbm, masked_hbm, table_hbm, gain_hbm, resid_hbm, normed_hbm,
    given_ref, kept_ref,
    lengths_ref, ids_ref, masked_ref, table_ref, gain_ref, resid_ref, normed_ref,
    center_ref, slope_gain_ref, total_ref, resid_row_ref, flat_ref, small_sem, resid_sem, normed_sem,
):
    small_copies = [
        pltpu.make_async_copy(source, target, small_sem.at[i])
        for i, (source, target) in enumerate(
            (
                (table_hbm, table_ref),
                (lengths_hbm, lengths_ref),
                (masked_hbm, masked_ref),
                (ids_hbm, ids_ref),
                (gain_hbm, gain_ref),
            )
        )
    ]
    resid_copy = pltpu.make_async_copy(resid_hbm, resid_ref, resid_sem)
    normed_copy = pltpu.make_async_copy(normed_hbm, normed_ref, normed_sem)
    for copy in [*small_copies, resid_copy, normed_copy]:
        copy.start()
    for copy in small_copies:
        copy.wait()
    width = table_ref.shape[1]
    blocks = width // LANES
    live, weight = token_rows(lengths_ref, masked_ref)
    n, slots = VOCAB_USED, weight.shape[1]
    small = table_ref[0:n, :].astype(jnp.float32) * SHRINK
    mean = jnp.sum(small, axis=1, keepdims=True) / width
    small = small - mean
    spread = jnp.sum(small * small, axis=1, keepdims=True) / width
    variance = jnp.minimum(spread * SHRINK**-2, 1e38)
    unit = lax.rsqrt(variance + EPS)
    unscaled = (variance + EPS) * unit
    for at in range(0, width, WIDTH_STEP):
        columns = slice(at, at + WIDTH_STEP)
        centered = (table_ref[0:n, columns].astype(jnp.float32) * SHRINK - mean) * SHRINK**-1
        center_ref[:, columns] = centered
        slope_gain_ref[:, columns] = centered * unit * gain_ref[:, columns]

    hit = ids_ref[...] == lax.broadcasted_iota(jnp.int32, (n, slots), 0)
    weighted = jnp.where(hit, weight, 0.0)
    through = weighted * lax.rsqrt(weight * weight * variance + EPS)
    ratio = through * unscaled
    row = lax.broadcasted_iota(jnp.int32, (16, slots), 0)
    alive = jnp.where(row == 0, live, 0.0).astype(jnp.bfloat16)
    left_resid = jnp.concatenate([*split2(weighted), alive], axis=0)
    left_normed = jnp.concatenate(
        [*split2(through), *split2(through * ratio * ratio), alive], axis=0
    )

    mean_sum = jnp.zeros((n, LANES), jnp.float32)
    slope_sum = jnp.zeros((n, LANES), jnp.float32)
    resid_copy.wait()
    for at in range(0, width, WIDTH_STEP):
        columns = slice(at, at + WIDTH_STEP)
        from_resid = jnp.dot(left_resid, resid_ref[:, columns], preferred_element_type=jnp.float32)
        total_ref[:, columns] = sum2(from_resid, 0)
        resid_row_ref[:, columns] = from_resid[2 * n : 2 * n + 1]
    normed_copy.wait()
    for at in range(0, width, WIDTH_STEP):
        columns = slice(at, at + WIDTH_STEP)
        from_normed = jnp.dot(
            left_normed, normed_ref[:, columns], preferred_element_type=jnp.float32
        )
        passed = sum2(from_normed, 0)
        gained = passed * gain_ref[:, columns]
        mean_sum += lane_fold(gained)
        slope_sum += lane_fold(slope_gain_ref[:, columns] * sum2(from_normed, 2 * n))
        total_ref[:, columns] += gained
        gain_grad = jnp.sum(center_ref[:, columns] * passed, axis=0, keepdims=True)
        row = lax.broadcasted_iota(jnp.int32, (SUBLANES, WIDTH_STEP), 0)
        layer = jnp.where(
            row == 1,
            resid_row_ref[:, columns],
            jnp.where(row == 2, gain_grad, jnp.where(row == 3, from_normed[4 * n : 4 * n + 1], 0.0)),
        )
        for k in range(WIDTH_STEP // LANES):
            at_row = n * blocks + at // LANES + k
            flat_ref[pl.ds(at_row, SUBLANES, stride=blocks), :] = layer[
                :, k * LANES : (k + 1) * LANES
            ]
    mean_sum = jnp.sum(mean_sum, axis=1, keepdims=True) / width
    slope = jnp.sum(slope_sum, axis=1, keepdims=True) / width * unit
    for k in range(blocks):
        columns = slice(k * LANES, (k + 1) * LANES)
        result = total_ref[:, columns] - mean_sum - center_ref[:, columns] * slope
        for tile in range(n // SUBLANES):
            rows = slice(tile * SUBLANES, (tile + 1) * SUBLANES)
            flat_ref[pl.ds(tile * SUBLANES * blocks + k, SUBLANES, stride=blocks), :] = result[rows]

    layer_row = (n + 1) * blocks

    def write(out_ref, core):
        for owner in range(OWNERS):
            for tile in range(PIECE * QUARTERS // SUBLANES):
                quarter, inner = divmod(tile, PIECE // SUBLANES)
                if quarter % 2 != core:
                    continue
                if tile == 0:
                    start = layer_row + owner * 15 // 2
                else:
                    start = owner * 165 // 2 + (tile - 1) * SUBLANES
                out_ref[PLANE.index(quarter // 2 * OWNERS + owner), pl.ds(inner * SUBLANES, SUBLANES), :] = (
                    flat_ref[pl.ds(start, SUBLANES), :]
                )

    core = lax.axis_index("core")
    for value in range(2):

        @pl.when(core == value)
        def _():
            write(kept_ref, value)
            write(given_ref, 1 - value)


def local_sums(lengths, ids, masked, table, gain, resid, normed):
    width = table.shape[1]
    operands = (lengths, ids[None], masked[None], table, gain[None], resid, normed)
    vmem = pl.BlockSpec(memory_space=pltpu.VMEM)
    hbm = pl.BlockSpec(memory_space=pltpu.HBM)
    out = pltpu.VMEM((2 * OWNERS, PIECE, LANES), jnp.float32)
    return pl.pallas_call(
        sums_kernel,
        out_shape=(out, out),
        in_specs=[hbm] * 7,
        out_specs=(vmem, vmem),
        scratch_shapes=[
            pltpu.SMEM(lengths.shape, jnp.int32),
            pltpu.VMEM((1, ids.shape[0]), jnp.int32),
            pltpu.VMEM((1, ids.shape[0]), jnp.int32),
            pltpu.VMEM(table.shape, table.dtype),
            pltpu.VMEM((1, width), jnp.float32),
            pltpu.VMEM(resid.shape, resid.dtype),
            pltpu.VMEM(normed.shape, normed.dtype),
            pltpu.VMEM((VOCAB_USED, width), jnp.float32),
            pltpu.VMEM((VOCAB_USED, width), jnp.float32),
            pltpu.VMEM((VOCAB_USED, width), jnp.float32),
            pltpu.VMEM((1, width), jnp.float32),
            pltpu.VMEM(((VOCAB_USED + SUBLANES) * width // LANES, LANES), jnp.float32),
            pltpu.SemaphoreType.DMA((5,)),
            pltpu.SemaphoreType.DMA,
            pltpu.SemaphoreType.DMA,
        ],
        compiler_params=pltpu.CompilerParams(vmem_limit_bytes=32 * 1024 * 1024),
        name="local_sums",
    )(*(pltpu.with_memory_space_constraint(operand, pltpu.HBM) for operand in operands))


def own_kernel(pieces_ref, layer_ref, embed_ref):
    half = LANES // 2
    odd = (lax.axis_index("y") & 1) == 1
    tiles = [
        pieces_ref[tile * SUBLANES // PIECE, pl.ds(tile * SUBLANES % PIECE, SUBLANES), :]
        for tile in range(PIECE * QUARTERS // SUBLANES)
    ]
    rolled = [pltpu.roll(tile, half, 1) for tile in tiles]
    lane = lax.broadcasted_iota(jnp.int32, (SUBLANES, LANES), 1)
    row = lax.broadcasted_iota(jnp.int32, (SUBLANES, LANES), 0)
    pieces = []
    for at, tile in enumerate(tiles):
        after = rolled[min(at + 1, len(tiles) - 1)]
        below = jnp.where(row == SUBLANES - 1, after[0:1], pltpu.roll(rolled[at], SUBLANES - 1, 0))
        pieces.append(jnp.where(odd, jnp.where(lane < half, rolled[at], below), tile))
    size = SUBLANES * LANES
    layer_ref[...] = pieces[0].reshape(size)[: layer_ref.shape[0]]
    for at, piece in enumerate(pieces[1:]):
        count = min(size, embed_ref.shape[0] - at * size)
        embed_ref[pl.ds(at * size, count)] = piece.reshape(size)[:count]


def own_blocks(pieces, layer, embed):
    vmem = pl.BlockSpec(memory_space=pltpu.VMEM)
    return pl.pallas_call(
        own_kernel,
        out_shape=(
            jax.ShapeDtypeStruct((layer,), jnp.float32),
            jax.ShapeDtypeStruct((embed,), jnp.float32),
        ),
        in_specs=[vmem],
        out_specs=(vmem, vmem),
        compiler_params=pltpu.CompilerParams(vmem_limit_bytes=4 * 1024 * 1024),
        name="own_blocks",
    )(pieces)


def to_all(block, axes, order):
    sent = jnp.broadcast_to(block[None], (len(order), *block.shape))
    return lax.all_to_all(sent, axes, 0, 0, axis_index_groups=[order], tiled=True)


def on_device(lengths, ids, masked, table, gain, resid, normed):
    given, kept = local_sums(lengths, ids, masked, table, gain, resid, normed)
    both = lax.all_gather(given, "core")
    pair = kept + lax.dynamic_index_in_dim(both, 1 - lax.axis_index("core"), 0, False)
    piece = jnp.sum(lax.all_to_all(pair, ("xh", "xl", "y"), 0, 0, axis_index_groups=[PLANE], tiled=True), axis=0)
    piece = jnp.sum(to_all(piece, "z", PLANES), axis=0)
    pieces = lax.all_gather(piece, ("xh", "core"))
    return own_blocks(
        pieces, 3 * table.shape[1] // OWNERS, table.shape[0] * table.shape[1] // OWNERS
    )


def solution(mesh):
    fine = Mesh(mesh.devices.reshape(12, 2, 2, 2, 8), HOLDERS)
    in_specs = (
        P(HOLDERS, None),
        P(HOLDERS),
        P(HOLDERS),
        P(),
        P(),
        P(HOLDERS, None),
        P(HOLDERS, None),
    )
    owners = P(("xl", "y"))
    return jax.shard_map(
        on_device, mesh=fine, in_specs=in_specs, out_specs=(owners, owners), check_vma=False
    )
```
